128 devices in a mesh: dp: 16 (over x, z), centre: 8 (over y, core).
Axes of the slice: x: 4, y: 4, z: 4, core: 2. Of those that a mesh axis runs over, the one named last changes fastest.
Arguments:
- pool: bfloat16 [65536, 1024], P('dp'), may hold values from -6 to 6
- sample_idx: int32 [32768], P('dp'), may hold values from 0 to 4095
- assign: int32 [32768], P('dp'), may hold values from 0 to 31, as said below
- counts: int32 [32], P('centre'), may hold values from 256 to 2048
- old_centres: float32 [32, 1024], P('centre', 'dp'), may hold values from -6 to 6
- precond: bfloat16 [32, 1024, 1024], P('centre', 'dp'), may hold values from -1 to 1
Outputs:
- new_centres: float32 [32, 1024], P('centre', 'dp')
- row_loss: float32 [32768], P('dp')
The draws below stay inside these ranges and needn't reach their ends.
Inputs may be any that keep to these rules, and one draw needn't show every extreme that they name: `assign`: in each aligned block of 2048 rows, no partition is named by more than 128 rows, and one partition, the same in every block, is named by exactly 128 rows.
All inputs are finite; a program needn't handle non-finite values.
Results may differ from the reference program's by a relative error of at most 0.0003.
Values may be sent and summed in bfloat16 or wider, within the bound.
A program may use at most 128 MiB of HBM per device.

```python
import math
import jax
import jax.numpy as jnp
from jax import lax

D = 1024
ROW_DEV = 2048
POOL_DEV = 4096
SWEEPS = 3
ROWS = 32768
POOL = 65536
PART_TOTAL = 32
CAP = 128
N_DP = 16


def draw_assign(key, part):
    key = jax.random.fold_in(key, 11)
    key_full, key_bias, key_blocks = jax.random.split(key, 3)
    full_part = jax.random.randint(key_full, (), 0, PART_TOTAL)
    bias = jax.random.randint(key_bias, (PART_TOTAL,), 0, 4) * 2048
    slot_total = PART_TOTAL * CAP
    slot_part = jnp.repeat(jnp.arange(PART_TOTAL, dtype=jnp.int32), CAP, total_repeat_length=slot_total)
    slot_ident = jnp.arange(slot_total, dtype=jnp.int32)

    def one_block(block_key):
        key_score, key_perm = jax.random.split(block_key)
        raw_score = jax.random.randint(key_score, (slot_total,), 0, 4096)
        score_value = (raw_score + bias[slot_part]) * slot_total + slot_ident
        score_value = jnp.where(slot_part == full_part, slot_ident - slot_total, score_value)
        order = jnp.argsort(score_value, stable=True)
        picked = slot_part[order[:ROW_DEV]]
        shuffle = jax.random.permutation(key_perm, ROW_DEV)
        return picked[shuffle]
    block_keys = jax.random.split(key_blocks, ROWS // ROW_DEV)
    return jax.vmap(one_block)(block_keys).reshape(ROWS).astype(jnp.int32)


def draw_precond(key, part):
    key = jax.random.fold_in(key, 23)
    key_diag, key_noise = jax.random.split(key)
    spread_level = 0.2 / D ** 0.5
    diag_gain = jax.random.uniform(key_diag, (PART_TOTAL, D), jnp.float32, 0.7, 0.9)
    noise = jax.random.normal(key_noise, (PART_TOTAL, D, D), jnp.float32) * spread_level
    identity = jnp.eye(D, dtype=jnp.float32)
    matrix = noise + identity[None, :, :] * diag_gain[:, :, None]
    return matrix.astype(jnp.bfloat16)


def place_ends(array, rng, smallest, top_value):
    place = [jax.random.randint(jax.random.fold_in(rng, axis), (), 0, length) for axis, length in enumerate(array.shape)]
    widest = array.shape.index(max(array.shape))
    neighbour = place[:widest] + [(place[widest] + 1) % array.shape[widest]] + place[widest + 1:]
    return array.at[tuple(place)].set(smallest).at[tuple(neighbour)].set(top_value)


def block_scale(key, extent, pieces, low, high):
    factor_of, own = 1.0, jax.random.fold_in(key, 6)
    for position, parts in pieces:
        heights = jnp.exp(jax.random.uniform(jax.random.fold_in(own, position), (parts,), jnp.float32, low / len(pieces), high / len(pieces)))
        factor_of = factor_of * jnp.repeat(heights, extent[position] // parts).reshape([-1 if axis == position else 1 for axis in range(len(extent))])
    return factor_of


def centred(key, dims, scale, limit, cuts=(), kind=jnp.bfloat16):
    factor_of = block_scale(key, dims, cuts, -0.22, 0.18) if cuts else 1.0
    array = jax.random.normal(key, dims, jnp.float32) * scale * factor_of
    return jnp.minimum(jnp.maximum(array, -limit), limit).astype(kind)


def setup_inputs(seed: int = 0) -> dict:
    keys = jax.random.split(jax.random.key(seed), 7)
    pool = centred(keys[0], (POOL, D), 1.0, 6.0, ((0, 16),))
    sample_idx = place_ends(jax.random.randint(keys[1], (ROWS,), 0, POOL_DEV), jax.random.fold_in(keys[1], 1), 0, POOL_DEV - 1).astype(jnp.int32)
    assign = draw_assign(jax.random.fold_in(keys[6], 71), 0)
    counts = place_ends(jax.random.randint(keys[3], (PART_TOTAL,), 256, 2049), jax.random.fold_in(keys[3], 1), 256, 2048).astype(jnp.int32)
    old_centres = centred(keys[4], (PART_TOTAL, D), 1.0, 6.0, ((0, 8), (1, 16)), jnp.float32)
    precond = draw_precond(jax.random.fold_in(keys[6], 71), 0)
    return {"pool": pool, "sample_idx": sample_idx, "assign": assign, "counts": counts, "old_centres": old_centres, "precond": precond}


THRESHOLD = 0.4
EPSILON = 1e-06

def reference(pool, sample_idx, assign, counts, old_centres, precond):
    aniso = (D - 1) * THRESHOLD ** 2 / (1 - THRESHOLD ** 2)
    base_rows = jnp.arange(ROWS, dtype=jnp.int32) // ROW_DEV * POOL_DEV + sample_idx.astype(jnp.int32)
    slab_rows = jnp.take(pool, base_rows, axis=0)
    slab_float = slab_rows.astype(jnp.float32)
    inv_norm = lax.rsqrt(lax.optimization_barrier(jnp.mean(slab_float * slab_float, axis=1, keepdims=True)) + EPSILON) / math.sqrt(D)
    unit_float = slab_float * inv_norm
    unit_rows = unit_float.astype(jnp.bfloat16)
    padded_unit = jnp.concatenate([unit_rows, jnp.zeros((1, D), jnp.bfloat16)], axis=0)
    padded_slab = jnp.concatenate([slab_rows, jnp.zeros((1, D), jnp.bfloat16)], axis=0)
    identity = jnp.eye(D, dtype=jnp.float32)
    highest = lax.Precision.HIGHEST
    mean_load = ROWS / PART_TOTAL * (D + aniso - 1.0) / D

    def solve_part(index):
        chosen_mask = assign == index
        member_rows = jnp.nonzero(chosen_mask, size=CAP * N_DP, fill_value=ROWS)[0].astype(jnp.int32)
        picked = jnp.take(padded_unit, member_rows, axis=0)
        outer_sum = jnp.dot(picked.T, picked, preferred_element_type=jnp.float32)
        picked_slab = jnp.take(padded_slab, member_rows, axis=0).astype(jnp.float32)
        member_count = jnp.sum(chosen_mask.astype(jnp.float32))
        prior = counts[index].astype(jnp.float32)
        gram = (aniso - 1.0) * outer_sum + (member_count + prior) * identity
        moment = aniso * lax.optimization_barrier(jnp.sum(picked_slab, axis=0)) + prior * old_centres[index]
        diag_mean = prior + mean_load
        gram_norm = gram / diag_mean
        moment_norm = moment / diag_mean
        inverse = precond[index].astype(jnp.float32)
        centre = jnp.dot(inverse, moment_norm, precision=highest)
        for sweep_step in range(SWEEPS):
            slack = moment_norm - jnp.dot(gram_norm, centre, precision=highest)
            centre = centre + jnp.dot(inverse, slack, precision=highest)
        return centre
    centres = lax.map(solve_part, jnp.arange(PART_TOTAL, dtype=jnp.int32))
    chosen = jnp.take(centres, assign.astype(jnp.int32), axis=0)
    deviation = slab_float - chosen
    along = lax.optimization_barrier(jnp.sum(deviation * unit_float, axis=1))
    row_loss = (lax.optimization_barrier(jnp.sum(deviation * deviation, axis=1)) + (aniso - 1.0) * along * along) / (aniso * D)
    return (centres, row_loss)
```

```python
import functools
import math

import jax
import jax.numpy as jnp
from jax import lax
from jax.experimental import pallas as pl
from jax.experimental.pallas import tpu as pltpu
from jax.sharding import PartitionSpec as P

D = 1024
SWEEPS = 3
CAP = 128
THRESHOLD = 0.4
EPSILON = 1e-06
ANISO = (D - 1) * THRESHOLD**2 / (1 - THRESHOLD**2)

LANES = 128
CHUNKS = D // LANES
SIDE = 4
COLS = 256
STEPS = D // COLS
MESH = pl.DeviceIdType.MESH


def iota(shape, axis):
    return lax.broadcasted_iota(jnp.int32, shape, axis)


def kernel(
    centre_count,
    mean_load,
    sample_ref,
    assign_ref,
    counts_ref,
    old_ref,
    precond_ref,
    pool_ref,
    centres_ref,
    loss_ref,
    pool_buf,
    picker,
    slot_of,
    picked,
    rows_in,
    unit,
    inv_own,
    inverse,
    moment_out,
    moment_in,
    line_out,
    line_in,
    whole_out,
    whole_in,
    loss_out,
    loss_in,
    pool_sem,
    own_sem,
    inv_send,
    inv_recv,
    row_send,
    row_recv,
    moment_sem,
    line_send,
    line_recv,
    whole_sem,
    loss_sem,
):
    place = lax.axis_index("dp")
    centre = lax.axis_index("centre")
    core = lax.rem(centre, 2)
    px, pz = place // SIDE, lax.rem(place, SIDE)
    group = (1 - core) * pz + core * px
    member = (1 - core) * px + core * pz

    def device(a, b):
        m, k = lax.rem(member + a, SIDE), lax.rem(group + b, SIDE)
        return (1 - core) * (m * SIDE + k) + core * (k * SIDE + m)

    def partition(b):
        return lax.rem(group + b, SIDE)

    def pool_copy(q):
        return pltpu.make_async_copy(
            pool_ref.at[:, pl.ds(q * COLS, COLS)], pool_buf.at[q], pool_sem.at[q]
        )

    for q in range(STEPS):
        pool_copy(q).start()
    own_inverse = pltpu.make_async_copy(precond_ref.at[group], inverse.at[0], own_sem)
    own_inverse.start()

    barrier = pltpu.get_barrier_semaphore()
    for a in range(SIDE):
        for b in range(SIDE):
            if a or b:
                pl.semaphore_signal(barrier, inc=1, device_id=(device(a, b), centre), device_id_type=MESH)
    for k in range(1, centre_count):
        pl.semaphore_signal(
            barrier, inc=1, device_id=(place, lax.rem(centre + k, centre_count)), device_id_type=MESH
        )

    first = centre * SIDE
    assign = assign_ref[...]
    masks = [(assign == first + k) for k in range(SIDE)]
    mask_all = jnp.concatenate([m.astype(jnp.float32) for m in masks], axis=0).astype(jnp.bfloat16)
    lane_row, lane_col = iota((LANES, LANES), 0), iota((LANES, LANES), 1)
    upper = (lane_row <= lane_col).astype(jnp.float32).astype(jnp.bfloat16)
    inside = jnp.dot(mask_all, upper, preferred_element_type=jnp.float32)
    ones = jnp.ones((LANES, LANES), jnp.bfloat16)
    totals = jnp.dot(mask_all, ones, preferred_element_type=jnp.float32)
    span = assign.shape[0]
    big_row, big_col = iota((SIDE * span, SIDE * span), 0), iota((SIDE * span, SIDE * span), 1)
    same = (big_row // span) == (big_col // span)
    before = (same & (big_col < big_row)).astype(jnp.float32).astype(jnp.bfloat16)
    ahead = jnp.dot(before, totals.astype(jnp.bfloat16), preferred_element_type=jnp.float32)
    rank = (inside + ahead).astype(jnp.int32) - 1
    for k in range(SIDE):
        slot_of[k * span : (k + 1) * span, :] = jnp.where(masks[k], rank[k * span : (k + 1) * span, :], -1)
    named = [jnp.sum(totals[k * span : (k + 1) * span, :], axis=0, keepdims=True) for k in range(SIDE)]

    sample = sample_ref[...] + 1
    slot_row = iota((CAP, LANES), 0)
    for k in range(SIDE):
        total = jnp.zeros((CAP, LANES), jnp.int32)
        for r in range(span):
            hit = slot_of[k * span + r : k * span + r + 1, :] == slot_row
            total += jnp.where(hit, sample[r : r + 1, :], 0)
        index = jnp.sum(total.astype(jnp.float32), axis=1, keepdims=True).astype(jnp.int32) - 1

        def pick(t, carry):
            hot = (iota((CAP, COLS), 1) + t * COLS) == index
            picker[t, k * CAP : (k + 1) * CAP, :] = hot.astype(jnp.float32).astype(jnp.bfloat16)
            return carry

        lax.fori_loop(0, picker.shape[0], pick, 0)

    pl.semaphore_wait(barrier, SIDE * SIDE - 1 + centre_count - 1)
    inverse_copies = []
    for b in range(1, SIDE):
        copy = pltpu.make_async_remote_copy(
            src_ref=precond_ref.at[partition(b)],
            dst_ref=inverse.at[b],
            send_sem=inv_send.at[b],
            recv_sem=inv_recv.at[b],
            device_id=(device(0, b), centre),
            device_id_type=MESH,
        )
        copy.start()
        inverse_copies.append(copy)

    sums = []
    row_copies = []
    for q in range(STEPS):
        pool_copy(q).wait()

        block = jnp.zeros((SIDE * CAP, COLS), jnp.float32)
        for t in range(picker.shape[0]):
            block += jnp.dot(
                picker[t], pool_buf[q, t * COLS : (t + 1) * COLS, :], preferred_element_type=jnp.float32
            )
        picked[q] = block.astype(jnp.bfloat16)
        sums.append(
            [jnp.sum(block[k * CAP : (k + 1) * CAP, :], axis=0, keepdims=True) for k in range(SIDE)]
        )
        for b in range(1, SIDE):
            copy = pltpu.make_async_remote_copy(
                src_ref=picked.at[q, pl.ds(partition(b) * CAP, CAP)],
                dst_ref=rows_in.at[b, q],
                send_sem=row_send.at[b, q],
                recv_sem=row_recv.at[b, q],
                device_id=(device(0, b), centre),
                device_id_type=MESH,
            )
            copy.start()
            row_copies.append(copy)

    tile_row = iota((CHUNKS, LANES), 0)
    half = lax.rem(place, 2)
    old = old_ref[...]
    twice = jnp.concatenate([old, old], axis=1)
    twice = jnp.where(iota(twice.shape, 1) // (LANES // 2) == half, twice, 0.0)
    for k in range(SIDE):
        rows = []
        for q in range(STEPS):
            for s in range(COLS // LANES):
                rows.append(sums[q][k][:, s * LANES : (s + 1) * LANES])
        tile = ANISO * jnp.concatenate(rows, axis=0)
        prior = counts_ref[k].astype(jnp.float32)
        tile += jnp.where(tile_row == place // 2, prior * twice[k : k + 1, :], 0.0)
        moment_out[k, 0] = tile
        moment_out[k, 1] = jnp.broadcast_to(named[k], (CHUNKS, LANES))
    for a in range(SIDE):
        for b in range(SIDE):
            if a or b:
                pltpu.make_async_remote_copy(
                    src_ref=moment_out.at[partition(b)],
                    dst_ref=moment_in.at[a * SIDE + b],
                    send_sem=moment_sem.at[0],
                    recv_sem=moment_sem.at[1],
                    device_id=(device(a, b), centre),
                    device_id_type=MESH,
                ).start()

    def own_norm(i, carry):
        rows = pl.ds(i * 32, 32)
        total = jnp.zeros((32, COLS), jnp.float32)
        for q in range(STEPS):
            x = picked[q, rows, :].astype(jnp.float32)
            total += x * x
        mean = jnp.sum(total, axis=1, keepdims=True) * (1.0 / D)
        inv_own[rows, :] = jnp.broadcast_to(lax.rsqrt(mean + EPSILON) / math.sqrt(D), (32, LANES))
        return carry

    lax.fori_loop(0, SIDE * CAP // 32, own_norm, 0)

    own_inverse.wait()
    for copy in inverse_copies:
        copy.wait_recv()
    arrived = moment_in.at[pl.ds(1, SIDE * SIDE - 1)]
    pltpu.make_async_copy(arrived, arrived, moment_sem.at[1]).wait()
    moment = moment_out[group, 0]
    count = moment_out[group, 1]
    for s in range(1, SIDE * SIDE):
        moment += moment_in[s, 0]
        count += moment_in[s, 1]
    prior = counts_ref[group].astype(jnp.float32)
    scale = prior + mean_load
    moment = moment / scale
    ridge = (count + prior) / scale

    block_row, block_lane = iota((64, LANES), 0), iota((64, LANES), 1)

    def apply_inverse(vector):
        tile = jnp.zeros((CHUNKS, LANES), jnp.float32)
        for b in range(SIDE):
            total = jnp.zeros((64, LANES), jnp.float32)
            for r in range(CHUNKS):
                w = inverse[b, :, r * LANES : (r + 1) * LANES].astype(jnp.float32)
                total += w * vector[r : r + 1, :]
            column = jnp.sum(total, axis=1, keepdims=True)
            home = device(0, SIDE - b)
            spread = jnp.where(block_lane == block_row + 64 * lax.rem(home, 2), column, 0.0)
            spread = jnp.sum(spread, axis=0, keepdims=True)
            tile += jnp.where(tile_row == home // 2, spread, 0.0)
        return tile

    def apply_outer(vector):
        def step(i, carry):
            rows = pl.ds(i * 32, 32)
            total = jnp.zeros((32, LANES), jnp.float32)
            pieces = []
            for r in range(CHUNKS):
                u = unit[rows, r * LANES : (r + 1) * LANES]
                pieces.append(u)
                total += u * vector[r : r + 1, :]
            along = jnp.sum(total, axis=1, keepdims=True)
            out = []
            for r in range(CHUNKS):
                v = pieces[r] * along
                out.append(carry[r] + ((v[0:8] + v[8:16]) + (v[16:24] + v[24:32])))
            return tuple(out)

        zero = tuple(jnp.zeros((8, LANES), jnp.float32) for _ in range(CHUNKS))
        parts = lax.fori_loop(0, SIDE * CAP // 32, step, zero, unroll=4)
        return jnp.concatenate([jnp.sum(p, axis=0, keepdims=True) for p in parts], axis=0)

    def line_sum(turn, tile):
        line_out[turn] = tile
        for a in range(1, SIDE):
            pltpu.make_async_remote_copy(
                src_ref=line_out.at[turn],
                dst_ref=line_in.at[turn, a],
                send_sem=line_send.at[turn],
                recv_sem=line_recv.at[turn],
                device_id=(device(a, 0), centre),
                device_id_type=MESH,
            ).start()
        here = line_in.at[turn, pl.ds(1, SIDE - 1)]

        def finish():
            pltpu.make_async_copy(here, here, line_recv.at[turn]).wait()
            return (tile + line_in[turn, 1]) + (line_in[turn, 2] + line_in[turn, 3])

        return finish

    finish = line_sum(0, apply_inverse(moment))

    for b in range(SIDE):
        if b:
            for q in range(STEPS):
                pltpu.make_async_copy(rows_in.at[b, q], rows_in.at[b, q], row_recv.at[b, q]).wait()

        def normalise(i, carry):
            x = []
            for q in range(STEPS):
                if b:
                    x.append(rows_in[b, q, pl.ds(i * 32, 32), :].astype(jnp.float32))
                else:
                    x.append(picked[q, pl.ds(group * CAP + i * 32, 32), :].astype(jnp.float32))
            total = jnp.zeros((32, COLS), jnp.float32)
            for q in range(STEPS):
                total += x[q] * x[q]
            mean = jnp.sum(total, axis=1, keepdims=True) * (1.0 / D)
            inv = lax.rsqrt(mean + EPSILON) / math.sqrt(D)
            for q in range(STEPS):
                u = (x[q] * inv).astype(jnp.bfloat16).astype(jnp.float32)
                unit[pl.ds(b * CAP + i * 32, 32), q * COLS : (q + 1) * COLS] = u
            return carry

        lax.fori_loop(0, CAP // 32, normalise, 0)

    vector = finish()
    for sweep in range(SWEEPS):
        product = line_sum(2 * sweep + 1, apply_outer(vector))()
        slack = moment - ((ANISO - 1.0) / scale * product + ridge * vector)
        change = apply_inverse(slack)
        if sweep < SWEEPS - 1:
            vector = vector + line_sum(2 * sweep + 2, change)()

    lane = iota((CHUNKS, LANES), 1)
    mine = jnp.zeros((CHUNKS, LANES), jnp.float32)
    for b in range(SIDE):
        home = device(0, b)
        mine += jnp.where((tile_row == home // 2) & (lane // 64 == lax.rem(home, 2)), vector, 0.0)
    whole_out[...] = mine + change
    for a in range(SIDE):
        for b in range(SIDE):
            if a or b:
                pltpu.make_async_remote_copy(
                    src_ref=whole_out,
                    dst_ref=whole_in.at[a * SIDE + b],
                    send_sem=whole_sem.at[0],
                    recv_sem=whole_sem.at[1],
                    device_id=(device(a, b), centre),
                    device_id_type=MESH,
                ).start()
    arrived = whole_in.at[pl.ds(1, SIDE * SIDE - 1)]
    pltpu.make_async_copy(arrived, arrived, whole_sem.at[1]).wait()

    losses = jnp.zeros((span, LANES), jnp.float32)
    centres = jnp.zeros((SIDE, LANES), jnp.float32)
    part_row = iota((SIDE, LANES), 0)
    span_row = iota((span, LANES), 0)
    for b in range(SIDE):
        k = lax.rem(group + SIDE - b, SIDE)
        tile = whole_out[...] if b == 0 else whole_in[b]
        for a in range(1, SIDE):
            tile = tile + whole_in[a * SIDE + b]
        block = jnp.sum(jnp.where(tile_row == place // 2, tile, 0.0), axis=0, keepdims=True)
        centres += jnp.where(part_row == k, block, 0.0)

        columns = []
        for i in range(CAP // 32):
            rows = pl.ds(k * CAP + i * 32, 32)
            square = jnp.zeros((32, LANES), jnp.float32)
            along = jnp.zeros((32, LANES), jnp.float32)
            for q in range(STEPS):
                x = picked[q, rows, :].astype(jnp.float32)
                for s in range(COLS // LANES):
                    r = q * (COLS // LANES) + s
                    xs = x[:, s * LANES : (s + 1) * LANES]
                    deviation = xs - tile[r : r + 1, :]
                    square += deviation * deviation
                    along += deviation * xs
            along = jnp.sum(along, axis=1, keepdims=True) * inv_own[rows, 0:1]
            square = jnp.sum(square, axis=1, keepdims=True)
            columns.append((square + (ANISO - 1.0) * along * along) / (ANISO * D))
        column = jnp.concatenate(columns, axis=0)
        slots = slot_of[pl.ds(k * span, span), :]
        for r in range(span):
            hit = slots[r : r + 1, :] == slot_row
            row = jnp.sum(jnp.where(hit, column, 0.0), axis=0, keepdims=True)
            losses += jnp.where(span_row == r, row, 0.0)

    loss_out[...] = losses
    for k in range(1, centre_count):
        pltpu.make_async_remote_copy(
            src_ref=loss_out,
            dst_ref=loss_in.at[k],
            send_sem=loss_sem.at[0],
            recv_sem=loss_sem.at[1],
            device_id=(place, lax.rem(centre + k, centre_count)),
            device_id_type=MESH,
        ).start()

    swapped = jnp.concatenate([centres[:, 64:], centres[:, :64]], axis=1)
    centres_ref[...] = jnp.where(half == 0, centres, swapped)[:, :64]
    for copy in inverse_copies + row_copies:
        copy.wait_send()
    sent = moment_in.at[pl.ds(1, SIDE * SIDE - 1)]
    pltpu.make_async_copy(sent, sent, moment_sem.at[0]).wait()
    for turn in range(2 * SWEEPS):
        sent = line_in.at[turn, pl.ds(1, SIDE - 1)]
        pltpu.make_async_copy(sent, sent, line_send.at[turn]).wait()
    sent = whole_in.at[pl.ds(1, SIDE * SIDE - 1)]
    pltpu.make_async_copy(sent, sent, whole_sem.at[0]).wait()
    if centre_count > 1:
        arrived = loss_in.at[pl.ds(1, centre_count - 1)]
        pltpu.make_async_copy(arrived, arrived, loss_sem.at[1]).wait()
        for k in range(1, centre_count):
            losses = losses + loss_in[k]
        pltpu.make_async_copy(arrived, arrived, loss_sem.at[0]).wait()
    loss_ref[...] = losses


def shards(pool, sample_idx, assign, counts, old_centres, precond):
    centre_count = lax.axis_size("centre")
    dp_count = lax.axis_size("dp")
    row_dev = sample_idx.shape[0]
    span = row_dev // LANES
    part_dev = counts.shape[0]
    mean_load = row_dev * dp_count / (part_dev * centre_count) * (D + ANISO - 1.0) / D
    pool_rows = pool.shape[0]
    f32, bf16 = jnp.float32, jnp.bfloat16
    vmem = pl.BlockSpec(memory_space=pltpu.VMEM)
    dma = pltpu.SemaphoreType.DMA
    plane = SIDE * SIDE
    centres, loss = pl.pallas_call(
        functools.partial(kernel, centre_count, mean_load),
        out_shape=(
            jax.ShapeDtypeStruct((part_dev, D // dp_count), f32),
            jax.ShapeDtypeStruct((span, LANES), f32),
        ),
        in_specs=[
            vmem,
            vmem,
            pl.BlockSpec(memory_space=pltpu.SMEM),
            vmem,
            pl.BlockSpec(memory_space=pl.ANY),
            pl.BlockSpec(memory_space=pl.ANY),
        ],
        out_specs=(vmem, vmem),
        scratch_shapes=[
            pltpu.VMEM((STEPS, pool_rows, COLS), bf16),
            pltpu.VMEM((pool_rows // COLS, SIDE * CAP, COLS), bf16),
            pltpu.VMEM((SIDE * span, LANES), jnp.int32),
            pltpu.VMEM((STEPS, SIDE * CAP, COLS), bf16),
            pltpu.VMEM((SIDE, STEPS, CAP, COLS), bf16),
            pltpu.VMEM((SIDE * CAP, D), f32),
            pltpu.VMEM((SIDE * CAP, LANES), f32),
            pltpu.VMEM((SIDE, D // dp_count, D), bf16),
            pltpu.VMEM((SIDE, 2, CHUNKS, LANES), f32),
            pltpu.VMEM((plane, 2, CHUNKS, LANES), f32),
            pltpu.VMEM((2 * SWEEPS, CHUNKS, LANES), f32),
            pltpu.VMEM((2 * SWEEPS, SIDE, CHUNKS, LANES), f32),
            pltpu.VMEM((CHUNKS, LANES), f32),
            pltpu.VMEM((plane, CHUNKS, LANES), f32),
            pltpu.VMEM((span, LANES), f32),
            pltpu.VMEM((centre_count, span, LANES), f32),
            dma((STEPS,)),
            dma,
            dma((SIDE,)),
            dma((SIDE,)),
            dma((SIDE, STEPS)),
            dma((SIDE, STEPS)),
            dma((2,)),
            dma((2 * SWEEPS,)),
            dma((2 * SWEEPS,)),
            dma((2,)),
            dma((2,)),
        ],
        compiler_params=pltpu.CompilerParams(
            collective_id=0, has_side_effects=True, vmem_limit_bytes=48 * 1024 * 1024
        ),
    )(sample_idx.reshape(span, LANES), assign.reshape(span, LANES), counts, old_centres, precond, pool)
    return centres, loss.reshape(row_dev)


def solution(mesh):
    return jax.shard_map(
        shards,
        mesh=mesh,
        in_specs=(
            P("dp", None),
            P("dp"),
            P("dp"),
            P("centre"),
            P("centre", "dp"),
            P("centre", "dp", None),
        ),
        out_specs=(P("centre", "dp"), P("dp")),
        check_vma=False,
    )
```

```python
import functools
import math

import jax
import jax.numpy as jnp
from jax import lax
from jax.experimental import pallas as pl
from jax.experimental.pallas import tpu as pltpu
from jax.sharding import PartitionSpec as P

D = 1024
SWEEPS = 3
CAP = 128
THRESHOLD = 0.4
EPSILON = 1e-06
ANISO = (D - 1) * THRESHOLD**2 / (1 - THRESHOLD**2)

LANES = 128
CHUNKS = D // LANES
SIDE = 4
PIECES = 8
MESH = pl.DeviceIdType.MESH


def iota(shape, axis):
    return lax.broadcasted_iota(jnp.int32, shape, axis)


def kernel(
    centre_count,
    mean_load,
    sample_hbm,
    assign_hbm,
    counts_hbm,
    old_hbm,
    precond_ref,
    pool_ref,
    centres_ref,
    loss_ref,
    sample_ref,
    assign_ref,
    counts_ref,
    old_ref,
    pool_buf,
    picker,
    slot_of,
    picked,
    rows_in,
    unit,
    inv_own,
    inverse,
    moment_out,
    moment_in,
    line_out,
    line_in,
    whole_out,
    whole_in,
    loss_out,
    loss_in,
    small_sem,
    pool_sem,
    own_sem,
    inv_send,
    inv_recv,
    row_send,
    row_recv,
    moment_sem,
    line_send,
    line_recv,
    whole_sem,
    loss_sem,
):
    place = lax.axis_index("dp")
    centre = lax.axis_index("centre")
    core = lax.rem(centre, 2)
    px, pz = place // SIDE, lax.rem(place, SIDE)
    group = (1 - core) * pz + core * px
    member = (1 - core) * px + core * pz

    def device(a, b):
        m, k = lax.rem(member + a, SIDE), lax.rem(group + b, SIDE)
        return (1 - core) * (m * SIDE + k) + core * (k * SIDE + m)

    def partition(b):
        return lax.rem(group + b, SIDE)

    def pool_copy(q):
        rows = pl.ds(q * (pool_ref.shape[0] // PIECES), pool_ref.shape[0] // PIECES)
        return pltpu.make_async_copy(pool_ref.at[rows], pool_buf.at[rows], pool_sem.at[q])

    small = [
        pltpu.make_async_copy(src, dst, small_sem.at[i])
        for i, (src, dst) in enumerate(
            [(assign_hbm, assign_ref), (sample_hbm, sample_ref), (counts_hbm, counts_ref), (old_hbm, old_ref)]
        )
    ]
    for copy in small:
        copy.start()
    for q in range(PIECES):
        pool_copy(q).start()
    own_inverse = pltpu.make_async_copy(precond_ref.at[group], inverse.at[0], own_sem)
    own_inverse.start()

    barrier = pltpu.get_barrier_semaphore()
    for a in range(SIDE):
        for b in range(SIDE):
            if a or b:
                pl.semaphore_signal(barrier, inc=1, device_id=(device(a, b), centre), device_id_type=MESH)
    for k in range(1, centre_count):
        pl.semaphore_signal(
            barrier, inc=1, device_id=(place, lax.rem(centre + k, centre_count)), device_id_type=MESH
        )

    first = centre * SIDE
    small[0].wait()
    assign = assign_ref[...]
    masks = [(assign == first + k) for k in range(SIDE)]
    mask_all = jnp.concatenate([m.astype(jnp.float32) for m in masks], axis=0).astype(jnp.bfloat16)
    lane_row, lane_col = iota((LANES, LANES), 0), iota((LANES, LANES), 1)
    upper = (lane_row <= lane_col).astype(jnp.float32).astype(jnp.bfloat16)
    inside = jnp.dot(mask_all, upper, preferred_element_type=jnp.float32)
    ones = jnp.ones((LANES, LANES), jnp.bfloat16)
    totals = jnp.dot(mask_all, ones, preferred_element_type=jnp.float32)
    span = assign.shape[0]
    big_row, big_col = iota((SIDE * span, SIDE * span), 0), iota((SIDE * span, SIDE * span), 1)
    same = (big_row // span) == (big_col // span)
    before = (same & (big_col < big_row)).astype(jnp.float32).astype(jnp.bfloat16)
    ahead = jnp.dot(before, totals.astype(jnp.bfloat16), preferred_element_type=jnp.float32)
    rank = (inside + ahead).astype(jnp.int32) - 1
    for k in range(SIDE):
        slot_of[k * span : (k + 1) * span, :] = jnp.where(masks[k], rank[k * span : (k + 1) * span, :], -1)
    named = [jnp.sum(totals[k * span : (k + 1) * span, :], axis=0, keepdims=True) for k in range(SIDE)]

    small[1].wait()
    sample = sample_ref[...] + 1
    slot_row = iota((CAP, LANES), 0)
    for k in range(SIDE):
        total = jnp.zeros((CAP, LANES), jnp.int32)
        for r in range(span):
            hit = slot_of[k * span + r : k * span + r + 1, :] == slot_row
            total += jnp.where(hit, sample[r : r + 1, :], 0)
        index = jnp.sum(total.astype(jnp.float32), axis=1, keepdims=True).astype(jnp.int32) - 1

        def pick(t, carry):
            hot = (iota((CAP, 256), 1) + t * 256) == index
            columns = pl.ds(pl.multiple_of(t * 256, 256), 256)
            picker[k * CAP : (k + 1) * CAP, columns] = hot.astype(jnp.float32).astype(jnp.bfloat16)
            return carry

        lax.fori_loop(0, picker.shape[1] // 256, pick, 0, unroll=4)

    pl.semaphore_wait(barrier, SIDE * SIDE - 1 + centre_count - 1)
    inverse_copies = []
    for b in range(1, SIDE):
        copy = pltpu.make_async_remote_copy(
            src_ref=precond_ref.at[partition(b)],
            dst_ref=inverse.at[b],
            send_sem=inv_send.at[b],
            recv_sem=inv_recv.at[b],
            device_id=(device(0, b), centre),
            device_id_type=MESH,
        )
        copy.start()
        inverse_copies.append(copy)
    for q in range(PIECES):
        pool_copy(q).wait()
    block = jnp.dot(picker[...], pool_buf[...], preferred_element_type=jnp.float32)
    picked[...] = block.astype(jnp.bfloat16)
    sums = [jnp.sum(block[k * CAP : (k + 1) * CAP, :], axis=0, keepdims=True) for k in range(SIDE)]

    tile_row = iota((CHUNKS, LANES), 0)
    half = lax.rem(place, 2)
    small[2].wait()
    small[3].wait()
    old = old_ref[...]
    twice = jnp.concatenate([old, old], axis=1)
    twice = jnp.where(iota(twice.shape, 1) // (LANES // 2) == half, twice, 0.0)
    for k in range(SIDE):
        rows = [sums[k][:, r * LANES : (r + 1) * LANES] for r in range(CHUNKS)]
        tile = ANISO * jnp.concatenate(rows, axis=0)
        prior = counts_ref[k].astype(jnp.float32)
        tile += jnp.where(tile_row == place // 2, prior * twice[k : k + 1, :], 0.0)
        moment_out[k, 0] = tile
        moment_out[k, 1] = jnp.broadcast_to(named[k], (CHUNKS, LANES))
    for a in range(SIDE):
        for b in range(SIDE):
            if a or b:
                pltpu.make_async_remote_copy(
                    src_ref=moment_out.at[partition(b)],
                    dst_ref=moment_in.at[a * SIDE + b],
                    send_sem=moment_sem.at[0],
                    recv_sem=moment_sem.at[1],
                    device_id=(device(a, b), centre),
                    device_id_type=MESH,
                ).start()

    row_copies = []
    for b in range(1, SIDE):
        copy = pltpu.make_async_remote_copy(
            src_ref=picked.at[pl.ds(partition(b) * CAP, CAP)],
            dst_ref=rows_in.at[b],
            send_sem=row_send.at[b],
            recv_sem=row_recv.at[b],
            device_id=(device(0, b), centre),
            device_id_type=MESH,
        )
        copy.start()
        row_copies.append(copy)

    def own_norm(i, carry):
        rows = pl.ds(i * 32, 32)
        total = jnp.zeros((32, LANES), jnp.float32)
        for r in range(CHUNKS):
            x = picked[rows, r * LANES : (r + 1) * LANES].astype(jnp.float32)
            total += x * x
        mean = jnp.sum(total, axis=1, keepdims=True) * (1.0 / D)
        inv_own[rows, :] = jnp.broadcast_to(lax.rsqrt(mean + EPSILON) / math.sqrt(D), (32, LANES))
        return carry

    lax.fori_loop(0, SIDE * CAP // 32, own_norm, 0)

    own_inverse.wait()
    for copy in inverse_copies:
        copy.wait_recv()
    arrived = moment_in.at[pl.ds(1, SIDE * SIDE - 1)]
    pltpu.make_async_copy(arrived, arrived, moment_sem.at[1]).wait()
    moment = moment_out[group, 0]
    count = moment_out[group, 1]
    for s in range(1, SIDE * SIDE):
        moment += moment_in[s, 0]
        count += moment_in[s, 1]
    prior = counts_ref[group].astype(jnp.float32)
    scale = prior + mean_load
    moment = moment / scale
    ridge = (count + prior) / scale

    block_row, block_lane = iota((64, LANES), 0), iota((64, LANES), 1)

    def apply_inverse(vector):
        tile = jnp.zeros((CHUNKS, LANES), jnp.float32)
        for b in range(SIDE):
            total = jnp.zeros((64, LANES), jnp.float32)
            for r in range(CHUNKS):
                w = inverse[b, :, r * LANES : (r + 1) * LANES].astype(jnp.float32)
                total += w * vector[r : r + 1, :]
            column = jnp.sum(total, axis=1, keepdims=True)
            home = device(0, SIDE - b)
            spread = jnp.where(block_lane == block_row + 64 * lax.rem(home, 2), column, 0.0)
            spread = jnp.sum(spread, axis=0, keepdims=True)
            tile += jnp.where(tile_row == home // 2, spread, 0.0)
        return tile

    def apply_outer(vector):
        alongs = []
        for i in range(SIDE * CAP // 32):
            total = jnp.zeros((32, LANES), jnp.float32)
            for r in range(CHUNKS):
                total += unit[i * 32 : (i + 1) * 32, r * LANES : (r + 1) * LANES] * vector[r : r + 1, :]
            alongs.append(jnp.sum(total, axis=1, keepdims=True))
        along = jnp.concatenate(alongs, axis=0)
        rows = []
        for r in range(CHUNKS):
            product = unit[:, r * LANES : (r + 1) * LANES] * along
            rows.append(jnp.sum(product, axis=0, keepdims=True))
        return jnp.concatenate(rows, axis=0)

    def line_sum(turn, tile):
        line_out[turn] = tile
        for a in range(1, SIDE):
            pltpu.make_async_remote_copy(
                src_ref=line_out.at[turn],
                dst_ref=line_in.at[turn, a],
                send_sem=line_send.at[turn],
                recv_sem=line_recv.at[turn],
                device_id=(device(a, 0), centre),
                device_id_type=MESH,
            ).start()
        here = line_in.at[turn, pl.ds(1, SIDE - 1)]

        def finish():
            pltpu.make_async_copy(here, here, line_recv.at[turn]).wait()
            return (tile + line_in[turn, 1]) + (line_in[turn, 2] + line_in[turn, 3])

        return finish

    finish = line_sum(0, apply_inverse(moment))

    for b in range(SIDE):
        if b:
            row_copies[b - 1].wait_recv()

        def normalise(i, carry):
            x = []
            for r in range(CHUNKS):
                columns = slice(r * LANES, (r + 1) * LANES)
                if b:
                    x.append(rows_in[b, pl.ds(i * 32, 32), columns].astype(jnp.float32))
                else:
                    x.append(picked[pl.ds(group * CAP + i * 32, 32), columns].astype(jnp.float32))
            total = jnp.zeros((32, LANES), jnp.float32)
            for r in range(CHUNKS):
                total += x[r] * x[r]
            mean = jnp.sum(total, axis=1, keepdims=True) * (1.0 / D)
            inv = lax.rsqrt(mean + EPSILON) / math.sqrt(D)
            for r in range(CHUNKS):
                u = (x[r] * inv).astype(jnp.bfloat16).astype(jnp.float32)
                unit[pl.ds(b * CAP + i * 32, 32), r * LANES : (r + 1) * LANES] = u
            return carry

        lax.fori_loop(0, CAP // 32, normalise, 0)

    vector = finish()
    for sweep in range(SWEEPS):
        product = line_sum(2 * sweep + 1, apply_outer(vector))()
        slack = moment - ((ANISO - 1.0) / scale * product + ridge * vector)
        change = apply_inverse(slack)
        if sweep < SWEEPS - 1:
            vector = vector + line_sum(2 * sweep + 2, change)()

    lane = iota((CHUNKS, LANES), 1)
    mine = jnp.zeros((CHUNKS, LANES), jnp.float32)
    for b in range(SIDE):
        home = device(0, b)
        mine += jnp.where((tile_row == home // 2) & (lane // 64 == lax.rem(home, 2)), vector, 0.0)
    whole_out[...] = mine + change
    for a in range(SIDE):
        for b in range(SIDE):
            if a or b:
                pltpu.make_async_remote_copy(
                    src_ref=whole_out,
                    dst_ref=whole_in.at[a * SIDE + b],
                    send_sem=whole_sem.at[0],
                    recv_sem=whole_sem.at[1],
                    device_id=(device(a, b), centre),
                    device_id_type=MESH,
                ).start()
    arrived = whole_in.at[pl.ds(1, SIDE * SIDE - 1)]
    pltpu.make_async_copy(arrived, arrived, whole_sem.at[1]).wait()

    losses = jnp.zeros((span, LANES), jnp.float32)
    centres = jnp.zeros((SIDE, LANES), jnp.float32)
    part_row = iota((SIDE, LANES), 0)
    for b in range(SIDE):
        k = lax.rem(group + SIDE - b, SIDE)
        tile = whole_out[...] if b == 0 else whole_in[b]
        for a in range(1, SIDE):
            tile = tile + whole_in[a * SIDE + b]
        block = jnp.sum(jnp.where(tile_row == place // 2, tile, 0.0), axis=0, keepdims=True)
        centres += jnp.where(part_row == k, block, 0.0)

        columns = []
        for i in range(CAP // 32):
            rows = pl.ds(k * CAP + i * 32, 32)
            square = jnp.zeros((32, LANES), jnp.float32)
            along = jnp.zeros((32, LANES), jnp.float32)
            for r in range(CHUNKS):
                x = picked[rows, r * LANES : (r + 1) * LANES].astype(jnp.float32)
                deviation = x - tile[r : r + 1, :]
                square += deviation * deviation
                along += deviation * x
            along = jnp.sum(along, axis=1, keepdims=True) * inv_own[rows, 0:1]
            square = jnp.sum(square, axis=1, keepdims=True)
            columns.append((square + (ANISO - 1.0) * along * along) / (ANISO * D))
        column = jnp.concatenate(columns, axis=0)
        table = jnp.sum(jnp.where(lane_row == lane_col, column, 0.0), axis=0, keepdims=True)
        table = jnp.broadcast_to(table, (span, LANES))
        slots = slot_of[pl.ds(k * span, span), :]
        found = jnp.take_along_axis(table, jnp.maximum(slots, 0), axis=1)
        losses += jnp.where(slots >= 0, found, 0.0)

    loss_out[...] = losses
    for k in range(1, centre_count):
        pltpu.make_async_remote_copy(
            src_ref=loss_out,
            dst_ref=loss_in.at[k],
            send_sem=loss_sem.at[0],
            recv_sem=loss_sem.at[1],
            device_id=(place, lax.rem(centre + k, centre_count)),
            device_id_type=MESH,
        ).start()

    swapped = jnp.concatenate([centres[:, 64:], centres[:, :64]], axis=1)
    centres_ref[...] = jnp.where(half == 0, centres, swapped)[:, :64]
    for copy in inverse_copies + row_copies:
        copy.wait_send()
    sent = moment_in.at[pl.ds(1, SIDE * SIDE - 1)]
    pltpu.make_async_copy(sent, sent, moment_sem.at[0]).wait()
    for turn in range(2 * SWEEPS):
        sent = line_in.at[turn, pl.ds(1, SIDE - 1)]
        pltpu.make_async_copy(sent, sent, line_send.at[turn]).wait()
    sent = whole_in.at[pl.ds(1, SIDE * SIDE - 1)]
    pltpu.make_async_copy(sent, sent, whole_sem.at[0]).wait()
    if centre_count > 1:
        arrived = loss_in.at[pl.ds(1, centre_count - 1)]
        pltpu.make_async_copy(arrived, arrived, loss_sem.at[1]).wait()
        for k in range(1, centre_count):
            losses = losses + loss_in[k]
        pltpu.make_async_copy(arrived, arrived, loss_sem.at[0]).wait()
    loss_ref[...] = losses


def shards(pool, sample_idx, assign, counts, old_centres, precond):
    centre_count = lax.axis_size("centre")
    dp_count = lax.axis_size("dp")
    row_dev = sample_idx.shape[0]
    span = row_dev // LANES
    part_dev = counts.shape[0]
    mean_load = row_dev * dp_count / (part_dev * centre_count) * (D + ANISO - 1.0) / D
    pool_rows = pool.shape[0]
    f32, bf16 = jnp.float32, jnp.bfloat16
    vmem = pl.BlockSpec(memory_space=pltpu.VMEM)
    dma = pltpu.SemaphoreType.DMA
    plane = SIDE * SIDE
    centres, loss = pl.pallas_call(
        functools.partial(kernel, centre_count, mean_load),
        out_shape=(
            jax.ShapeDtypeStruct((part_dev, D // dp_count), f32),
            jax.ShapeDtypeStruct((span, LANES), f32),
        ),
        in_specs=[pl.BlockSpec(memory_space=pltpu.HBM)] * 6,
        out_specs=(vmem, vmem),
        scratch_shapes=[
            pltpu.VMEM((span, LANES), jnp.int32),
            pltpu.VMEM((span, LANES), jnp.int32),
            pltpu.SMEM((part_dev,), jnp.int32),
            pltpu.VMEM((part_dev, D // dp_count), f32),
            pltpu.VMEM((pool_rows, D), bf16),
            pltpu.VMEM((SIDE * CAP, pool_rows), bf16),
            pltpu.VMEM((SIDE * span, LANES), jnp.int32),
            pltpu.VMEM((SIDE * CAP, D), bf16),
            pltpu.VMEM((SIDE, CAP, D), bf16),
            pltpu.VMEM((SIDE * CAP, D), f32),
            pltpu.VMEM((SIDE * CAP, LANES), f32),
            pltpu.VMEM((SIDE, D // dp_count, D), bf16),
            pltpu.VMEM((SIDE, 2, CHUNKS, LANES), f32),
            pltpu.VMEM((plane, 2, CHUNKS, LANES), f32),
            pltpu.VMEM((2 * SWEEPS, CHUNKS, LANES), f32),
            pltpu.VMEM((2 * SWEEPS, SIDE, CHUNKS, LANES), f32),
            pltpu.VMEM((CHUNKS, LANES), f32),
            pltpu.VMEM((plane, CHUNKS, LANES), f32),
            pltpu.VMEM((span, LANES), f32),
            pltpu.VMEM((centre_count, span, LANES), f32),
            dma((4,)),
            dma((PIECES,)),
            dma,
            dma((SIDE,)),
            dma((SIDE,)),
            dma((SIDE,)),
            dma((SIDE,)),
            dma((2,)),
            dma((2 * SWEEPS,)),
            dma((2 * SWEEPS,)),
            dma((2,)),
            dma((2,)),
        ],
        compiler_params=pltpu.CompilerParams(
            collective_id=0, has_side_effects=True, vmem_limit_bytes=64 * 1024 * 1024 - 65536
        ),
    )(sample_idx.reshape(span, LANES), assign.reshape(span, LANES), counts, old_centres, precond, pool)
    return centres, loss.reshape(row_dev)


def solution(mesh):
    return jax.shard_map(
        shards,
        mesh=mesh,
        in_specs=(
            P("dp", None),
            P("dp"),
            P("dp"),
            P("centre"),
            P("centre", "dp"),
            P("centre", "dp", None),
        ),
        out_specs=(P("centre", "dp"), P("dp")),
        check_vma=False,
    )
```

```python
import functools
import math

import jax
import jax.numpy as jnp
from jax import lax
from jax.experimental import pallas as pl
from jax.experimental.pallas import tpu as pltpu
from jax.sharding import PartitionSpec as P

D = 1024
SWEEPS = 3
CAP = 128
THRESHOLD = 0.4
EPSILON = 1e-06
ANISO = (D - 1) * THRESHOLD**2 / (1 - THRESHOLD**2)

LANES = 128
CHUNKS = D // LANES
SIDE = 4
PIECES = 8
HALF = D // 2
MESH = pl.DeviceIdType.MESH


def iota(shape, axis):
    return lax.broadcasted_iota(jnp.int32, shape, axis)


def kernel(
    centre_count,
    mean_load,
    sample_hbm,
    assign_hbm,
    counts_hbm,
    old_hbm,
    precond_ref,
    pool_ref,
    centres_ref,
    loss_ref,
    sample_ref,
    assign_ref,
    counts_ref,
    old_ref,
    pool_buf,
    picker,
    times,
    slot_of,
    picked,
    rows_in,
    unit,
    inv_own,
    inverse,
    moment_out,
    moment_in,
    line_out,
    line_in,
    whole_out,
    whole_in,
    loss_out,
    loss_in,
    small_sem,
    pool_sem,
    own_sem,
    inv_send,
    inv_recv,
    row_send,
    row_recv,
    moment_sem,
    line_send,
    line_recv,
    whole_sem,
    loss_sem,
):
    place = lax.axis_index("dp")
    centre = lax.axis_index("centre")
    core = lax.rem(centre, 2)
    px, pz = place // SIDE, lax.rem(place, SIDE)
    group = (1 - core) * pz + core * px
    member = (1 - core) * px + core * pz

    def device(a, b):
        m, k = lax.rem(member + a, SIDE), lax.rem(group + b, SIDE)
        return (1 - core) * (m * SIDE + k) + core * (k * SIDE + m)

    def partition(b):
        return lax.rem(group + b, SIDE)

    def pool_copy(q):
        rows = pl.ds(q * (pool_ref.shape[0] // PIECES), pool_ref.shape[0] // PIECES)
        return pltpu.make_async_copy(pool_ref.at[rows], pool_buf.at[rows], pool_sem.at[q])

    small = [
        pltpu.make_async_copy(src, dst, small_sem.at[i])
        for i, (src, dst) in enumerate(
            [(assign_hbm, assign_ref), (sample_hbm, sample_ref), (counts_hbm, counts_ref), (old_hbm, old_ref)]
        )
    ]
    for copy in small:
        copy.start()
    for q in range(PIECES):
        pool_copy(q).start()
    own_inverse = pltpu.make_async_copy(precond_ref.at[group], inverse.at[0], own_sem)
    own_inverse.start()

    barrier = pltpu.get_barrier_semaphore()
    for a in range(SIDE):
        for b in range(SIDE):
            if a or b:
                pl.semaphore_signal(barrier, inc=1, device_id=(device(a, b), centre), device_id_type=MESH)
    for k in range(1, centre_count):
        pl.semaphore_signal(
            barrier, inc=1, device_id=(place, lax.rem(centre + k, centre_count)), device_id_type=MESH
        )

    first = centre * SIDE
    small[0].wait()
    assign = assign_ref[...]
    masks = [(assign == first + k) for k in range(SIDE)]
    mask_all = jnp.concatenate([m.astype(jnp.float32) for m in masks], axis=0).astype(jnp.bfloat16)
    lane_row, lane_col = iota((LANES, LANES), 0), iota((LANES, LANES), 1)
    upper = (lane_row <= lane_col).astype(jnp.float32).astype(jnp.bfloat16)
    inside = jnp.dot(mask_all, upper, preferred_element_type=jnp.float32)
    ones = jnp.ones((LANES, LANES), jnp.bfloat16)
    totals = jnp.dot(mask_all, ones, preferred_element_type=jnp.float32)
    span = assign.shape[0]
    big_row, big_col = iota((SIDE * span, SIDE * span), 0), iota((SIDE * span, SIDE * span), 1)
    same = (big_row // span) == (big_col // span)
    before = (same & (big_col < big_row)).astype(jnp.float32).astype(jnp.bfloat16)
    ahead = jnp.dot(before, totals.astype(jnp.bfloat16), preferred_element_type=jnp.float32)
    rank = (inside + ahead).astype(jnp.int32) - 1
    for k in range(SIDE):
        slot_of[k] = jnp.where(masks[k], rank[k * span : (k + 1) * span, :], -1)
    named = [jnp.sum(totals[k * span : (k + 1) * span, :], axis=0, keepdims=True) for k in range(SIDE)]

    small[1].wait()
    sample = sample_ref[...] + 1
    slot_row = iota((CAP, LANES), 0)
    times[...] = jnp.zeros(times.shape, jnp.float32)
    for k in range(SIDE):
        total = jnp.zeros((CAP, LANES), jnp.int32)
        for r in range(span):
            hit = slot_of[k, r : r + 1, :] == slot_row
            total += jnp.where(hit, sample[r : r + 1, :], 0)
        index = jnp.sum(total.astype(jnp.float32), axis=1, keepdims=True).astype(jnp.int32) - 1

        def pick(t, carry):
            hot = (iota((CAP, 256), 1) + t * 256) == index
            columns = pl.ds(pl.multiple_of(t * 256, 256), 256)
            hot = hot.astype(jnp.float32)
            picker[k * CAP : (k + 1) * CAP, columns] = hot.astype(jnp.bfloat16)
            times[k : k + 1, columns] = jnp.sum(hot, axis=0, keepdims=True)
            return carry

        lax.fori_loop(0, picker.shape[1] // 256, pick, 0, unroll=4)

    pl.semaphore_wait(barrier, SIDE * SIDE - 1 + centre_count - 1)
    inverse_copies = []
    for b in range(1, SIDE):
        copy = pltpu.make_async_remote_copy(
            src_ref=precond_ref.at[partition(b)],
            dst_ref=inverse.at[b],
            send_sem=inv_send.at[b],
            recv_sem=inv_recv.at[b],
            device_id=(device(0, b), centre),
            device_id_type=MESH,
        )
        copy.start()
        inverse_copies.append(copy)
    for q in range(PIECES):
        pool_copy(q).wait()
    tile_row = iota((CHUNKS, LANES), 0)
    half = lax.rem(place, 2)
    small[2].wait()
    small[3].wait()
    old = old_ref[...]
    sums = jnp.dot(times[...].astype(jnp.bfloat16), pool_buf[...], preferred_element_type=jnp.float32)
    twice = jnp.concatenate([old, old], axis=1)
    twice = jnp.where(iota(twice.shape, 1) // (LANES // 2) == half, twice, 0.0)
    for k in range(SIDE):
        rows = [sums[k : k + 1, r * LANES : (r + 1) * LANES] for r in range(CHUNKS)]
        tile = ANISO * jnp.concatenate(rows, axis=0)
        prior = counts_ref[k].astype(jnp.float32)
        tile += jnp.where(tile_row == place // 2, prior * twice[k : k + 1, :], 0.0)
        moment_out[k, 0] = tile
        moment_out[k, 1] = jnp.broadcast_to(named[k], (CHUNKS, LANES))
    for a in range(SIDE):
        for b in range(SIDE):
            if a or b:
                pltpu.make_async_remote_copy(
                    src_ref=moment_out.at[partition(b)],
                    dst_ref=moment_in.at[a * SIDE + b],
                    send_sem=moment_sem.at[0],
                    recv_sem=moment_sem.at[1],
                    device_id=(device(a, b), centre),
                    device_id_type=MESH,
                ).start()

    row_copies = []
    for h in range(2):
        block = jnp.dot(picker[...], pool_buf[:, h * HALF : (h + 1) * HALF], preferred_element_type=jnp.float32)
        picked[h] = block.astype(jnp.bfloat16).reshape(SIDE, CAP, HALF)
        for b in range(1, SIDE):
            copy = pltpu.make_async_remote_copy(
                src_ref=picked.at[h, partition(b)],
                dst_ref=rows_in.at[h, b],
                send_sem=row_send.at[h, b],
                recv_sem=row_recv.at[h, b],
                device_id=(device(0, b), centre),
                device_id_type=MESH,
            )
            copy.start()
            row_copies.append(copy)

    def piece(ref, part, rows, r):
        start = r % (CHUNKS // 2) * LANES
        return ref[r // (CHUNKS // 2), part, rows, start : start + LANES].astype(jnp.float32)

    def own_norm(k, carry):
        for i in range(CAP // 32):
            rows = slice(i * 32, (i + 1) * 32)
            total = jnp.zeros((32, LANES), jnp.float32)
            for r in range(CHUNKS):
                x = piece(picked, k, rows, r)
                total += x * x
            mean = jnp.sum(total, axis=1, keepdims=True) * (1.0 / D)
            inv_own[k, rows, :] = jnp.broadcast_to(lax.rsqrt(mean + EPSILON) / math.sqrt(D), (32, LANES))
        return carry

    lax.fori_loop(0, SIDE, own_norm, 0)

    own_inverse.wait()
    for copy in inverse_copies:
        copy.wait_recv()
    arrived = moment_in.at[pl.ds(1, SIDE * SIDE - 1)]
    pltpu.make_async_copy(arrived, arrived, moment_sem.at[1]).wait()
    moment = moment_out[group, 0]
    count = moment_out[group, 1]
    for s in range(1, SIDE * SIDE):
        moment += moment_in[s, 0]
        count += moment_in[s, 1]
    prior = counts_ref[group].astype(jnp.float32)
    scale = prior + mean_load
    moment = moment / scale
    ridge = (count + prior) / scale

    block_row, block_lane = iota((64, LANES), 0), iota((64, LANES), 1)

    def apply_inverse(vector):
        tile = jnp.zeros((CHUNKS, LANES), jnp.float32)
        for b in range(SIDE):
            total = jnp.zeros((64, LANES), jnp.float32)
            for r in range(CHUNKS):
                w = inverse[b, :, r * LANES : (r + 1) * LANES].astype(jnp.float32)
                total += w * vector[r : r + 1, :]
            column = jnp.sum(total, axis=1, keepdims=True)
            home = device(0, SIDE - b)
            spread = jnp.where(block_lane == block_row + 64 * lax.rem(home, 2), column, 0.0)
            spread = jnp.sum(spread, axis=0, keepdims=True)
            tile += jnp.where(tile_row == home // 2, spread, 0.0)
        return tile

    def apply_outer(vector):
        alongs = []
        for i in range(SIDE * CAP // 32):
            total = jnp.zeros((32, LANES), jnp.float32)
            for r in range(CHUNKS):
                total += unit[i * 32 : (i + 1) * 32, r * LANES : (r + 1) * LANES] * vector[r : r + 1, :]
            alongs.append(jnp.sum(total, axis=1, keepdims=True))
        along = jnp.concatenate(alongs, axis=0)
        rows = []
        for r in range(CHUNKS):
            product = unit[:, r * LANES : (r + 1) * LANES] * along
            rows.append(jnp.sum(product, axis=0, keepdims=True))
        return jnp.concatenate(rows, axis=0)

    def line_sum(turn, tile):
        line_out[turn] = tile
        for a in range(1, SIDE):
            pltpu.make_async_remote_copy(
                src_ref=line_out.at[turn],
                dst_ref=line_in.at[turn, a],
                send_sem=line_send.at[turn],
                recv_sem=line_recv.at[turn],
                device_id=(device(a, 0), centre),
                device_id_type=MESH,
            ).start()
        here = line_in.at[turn, pl.ds(1, SIDE - 1)]

        def finish():
            pltpu.make_async_copy(here, here, line_recv.at[turn]).wait()
            return (tile + line_in[turn, 1]) + (line_in[turn, 2] + line_in[turn, 3])

        return finish

    finish = line_sum(0, apply_inverse(moment))

    for b in range(SIDE):
        if b:
            row_copies[b - 1].wait_recv()
            row_copies[b + SIDE - 2].wait_recv()

        for i in range(CAP // 32):
            rows = slice(i * 32, (i + 1) * 32)
            x = []
            for r in range(CHUNKS):
                x.append(piece(rows_in, b, rows, r) if b else piece(picked, group, rows, r))
            total = jnp.zeros((32, LANES), jnp.float32)
            for r in range(CHUNKS):
                total += x[r] * x[r]
            mean = jnp.sum(total, axis=1, keepdims=True) * (1.0 / D)
            inv = lax.rsqrt(mean + EPSILON) / math.sqrt(D)
            for r in range(CHUNKS):
                u = (x[r] * inv).astype(jnp.bfloat16).astype(jnp.float32)
                unit[b * CAP + i * 32 : b * CAP + (i + 1) * 32, r * LANES : (r + 1) * LANES] = u

    vector = finish()
    for sweep in range(SWEEPS):
        product = line_sum(2 * sweep + 1, apply_outer(vector))()
        slack = moment - ((ANISO - 1.0) / scale * product + ridge * vector)
        change = apply_inverse(slack)
        if sweep < SWEEPS - 1:
            vector = vector + line_sum(2 * sweep + 2, change)()

    lane = iota((CHUNKS, LANES), 1)
    mine = jnp.zeros((CHUNKS, LANES), jnp.float32)
    for b in range(SIDE):
        home = device(0, b)
        mine += jnp.where((tile_row == home // 2) & (lane // 64 == lax.rem(home, 2)), vector, 0.0)
    whole_out[...] = mine + change
    for a in range(SIDE):
        for b in range(SIDE):
            if a or b:
                pltpu.make_async_remote_copy(
                    src_ref=whole_out,
                    dst_ref=whole_in.at[a * SIDE + b],
                    send_sem=whole_sem.at[0],
                    recv_sem=whole_sem.at[1],
                    device_id=(device(a, b), centre),
                    device_id_type=MESH,
                ).start()
    arrived = whole_in.at[pl.ds(1, SIDE * SIDE - 1)]
    pltpu.make_async_copy(arrived, arrived, whole_sem.at[1]).wait()

    losses = jnp.zeros((span, LANES), jnp.float32)
    centres = jnp.zeros((SIDE, LANES), jnp.float32)
    part_row = iota((SIDE, LANES), 0)
    for b in range(SIDE):
        k = lax.rem(group + SIDE - b, SIDE)
        tile = whole_out[...] if b == 0 else whole_in[b]
        for a in range(1, SIDE):
            tile = tile + whole_in[a * SIDE + b]
        block = jnp.sum(jnp.where(tile_row == place // 2, tile, 0.0), axis=0, keepdims=True)
        centres += jnp.where(part_row == k, block, 0.0)

        columns = []
        for i in range(CAP // 32):
            rows = slice(i * 32, (i + 1) * 32)
            square = jnp.zeros((32, LANES), jnp.float32)
            along = jnp.zeros((32, LANES), jnp.float32)
            for r in range(CHUNKS):
                x = piece(picked, k, rows, r)
                deviation = x - tile[r : r + 1, :]
                square += deviation * deviation
                along += deviation * x
            along = jnp.sum(along, axis=1, keepdims=True) * inv_own[k, rows, 0:1]
            square = jnp.sum(square, axis=1, keepdims=True)
            columns.append((square + (ANISO - 1.0) * along * along) / (ANISO * D))
        column = jnp.concatenate(columns, axis=0)
        table = jnp.sum(jnp.where(lane_row == lane_col, column, 0.0), axis=0, keepdims=True)
        table = jnp.broadcast_to(table, (span, LANES))
        slots = slot_of[k]
        found = jnp.take_along_axis(table, jnp.maximum(slots, 0), axis=1)
        losses += jnp.where(slots >= 0, found, 0.0)

    loss_out[...] = losses
    for k in range(1, centre_count):
        pltpu.make_async_remote_copy(
            src_ref=loss_out,
            dst_ref=loss_in.at[k],
            send_sem=loss_sem.at[0],
            recv_sem=loss_sem.at[1],
            device_id=(place, lax.rem(centre + k, centre_count)),
            device_id_type=MESH,
        ).start()

    swapped = jnp.concatenate([centres[:, 64:], centres[:, :64]], axis=1)
    centres_ref[...] = jnp.where(half == 0, centres, swapped)[:, :64]
    for copy in inverse_copies + row_copies:
        copy.wait_send()
    sent = moment_in.at[pl.ds(1, SIDE * SIDE - 1)]
    pltpu.make_async_copy(sent, sent, moment_sem.at[0]).wait()
    for turn in range(2 * SWEEPS):
        sent = line_in.at[turn, pl.ds(1, SIDE - 1)]
        pltpu.make_async_copy(sent, sent, line_send.at[turn]).wait()
    sent = whole_in.at[pl.ds(1, SIDE * SIDE - 1)]
    pltpu.make_async_copy(sent, sent, whole_sem.at[0]).wait()
    if centre_count > 1:
        arrived = loss_in.at[pl.ds(1, centre_count - 1)]
        pltpu.make_async_copy(arrived, arrived, loss_sem.at[1]).wait()
        for k in range(1, centre_count):
            losses = losses + loss_in[k]
        pltpu.make_async_copy(arrived, arrived, loss_sem.at[0]).wait()
    loss_ref[...] = losses


def shards(pool, sample_idx, assign, counts, old_centres, precond):
    centre_count = lax.axis_size("centre")
    dp_count = lax.axis_size("dp")
    row_dev = sample_idx.shape[0]
    span = row_dev // LANES
    part_dev = counts.shape[0]
    mean_load = row_dev * dp_count / (part_dev * centre_count) * (D + ANISO - 1.0) / D
    pool_rows = pool.shape[0]
    f32, bf16 = jnp.float32, jnp.bfloat16
    vmem = pl.BlockSpec(memory_space=pltpu.VMEM)
    dma = pltpu.SemaphoreType.DMA
    plane = SIDE * SIDE
    centres, loss = pl.pallas_call(
        functools.partial(kernel, centre_count, mean_load),
        out_shape=(
            jax.ShapeDtypeStruct((part_dev, D // dp_count), f32),
            jax.ShapeDtypeStruct((span, LANES), f32),
        ),
        in_specs=[pl.BlockSpec(memory_space=pltpu.HBM)] * 6,
        out_specs=(vmem, vmem),
        scratch_shapes=[
            pltpu.VMEM((span, LANES), jnp.int32),
            pltpu.VMEM((span, LANES), jnp.int32),
            pltpu.SMEM((part_dev,), jnp.int32),
            pltpu.VMEM((part_dev, D // dp_count), f32),
            pltpu.VMEM((pool_rows, D), bf16),
            pltpu.VMEM((SIDE * CAP, pool_rows), bf16),
            pltpu.VMEM((8, pool_rows), f32),
            pltpu.VMEM((SIDE, span, LANES), jnp.int32),
            pltpu.VMEM((2, SIDE, CAP, HALF), bf16),
            pltpu.VMEM((2, SIDE, CAP, HALF), bf16),
            pltpu.VMEM((SIDE * CAP, D), f32),
            pltpu.VMEM((SIDE, CAP, LANES), f32),
            pltpu.VMEM((SIDE, D // dp_count, D), bf16),
            pltpu.VMEM((SIDE, 2, CHUNKS, LANES), f32),
            pltpu.VMEM((plane, 2, CHUNKS, LANES), f32),
            pltpu.VMEM((2 * SWEEPS, CHUNKS, LANES), f32),
            pltpu.VMEM((2 * SWEEPS, SIDE, CHUNKS, LANES), f32),
            pltpu.VMEM((CHUNKS, LANES), f32),
            pltpu.VMEM((plane, CHUNKS, LANES), f32),
            pltpu.VMEM((span, LANES), f32),
            pltpu.VMEM((centre_count, span, LANES), f32),
            dma((4,)),
            dma((PIECES,)),
            dma,
            dma((SIDE,)),
            dma((SIDE,)),
            dma((2, SIDE)),
            dma((2, SIDE)),
            dma((2,)),
            dma((2 * SWEEPS,)),
            dma((2 * SWEEPS,)),
            dma((2,)),
            dma((2,)),
        ],
        compiler_params=pltpu.CompilerParams(
            collective_id=0, has_side_effects=True, vmem_limit_bytes=48 * 1024 * 1024
        ),
    )(*(pltpu.with_memory_space_constraint(a, pltpu.HBM) for a in (sample_idx.reshape(span, LANES), assign.reshape(span, LANES), counts, old_centres, precond, pool)))
    return centres, loss.reshape(row_dev)


def solution(mesh):
    return jax.shard_map(
        shards,
        mesh=mesh,
        in_specs=(
            P("dp", None),
            P("dp"),
            P("dp"),
            P("centre"),
            P("centre", "dp"),
            P("centre", "dp", None),
        ),
        out_specs=(P("centre", "dp"), P("dp")),
        check_vma=False,
    )
```

```python
import functools
import math

import jax
import jax.numpy as jnp
from jax import lax
from jax.experimental import pallas as pl
from jax.experimental.pallas import tpu as pltpu
from jax.sharding import PartitionSpec as P

D = 1024
SWEEPS = 3
CAP = 128
THRESHOLD = 0.4
EPSILON = 1e-06
ANISO = (D - 1) * THRESHOLD**2 / (1 - THRESHOLD**2)

LANES = 128
CHUNKS = D // LANES
SIDE = 4
PIECES = 8
HALF = D // 2
MESH = pl.DeviceIdType.MESH


FAR = sorted(
    [(a, b) for a in range(SIDE) for b in range(SIDE) if a or b],
    key=lambda step: -sum(min(n, SIDE - n) for n in step),
)


def iota(shape, axis):
    return lax.broadcasted_iota(jnp.int32, shape, axis)


def kernel(
    centre_count,
    mean_load,
    sample_hbm,
    assign_hbm,
    counts_hbm,
    old_hbm,
    precond_ref,
    pool_ref,
    centres_ref,
    loss_ref,
    sample_ref,
    assign_ref,
    counts_ref,
    old_ref,
    pool_buf,
    picker,
    times,
    slot_of,
    picked,
    rows_in,
    unit,
    inv_own,
    inverse,
    moment_out,
    moment_in,
    count_out,
    count_in,
    line_out,
    line_in,
    whole_out,
    whole_in,
    loss_out,
    loss_in,
    small_sem,
    pool_sem,
    own_sem,
    inv_send,
    inv_recv,
    row_send,
    row_recv,
    moment_sem,
    count_send,
    count_recv,
    line_send,
    line_recv,
    whole_sem,
    loss_sem,
):
    place = lax.axis_index("dp")
    centre = lax.axis_index("centre")
    core = lax.rem(centre, 2)
    px, pz = place // SIDE, lax.rem(place, SIDE)
    group = (1 - core) * pz + core * px
    member = (1 - core) * px + core * pz

    def device(a, b):
        m, k = lax.rem(member + a, SIDE), lax.rem(group + b, SIDE)
        return (1 - core) * (m * SIDE + k) + core * (k * SIDE + m)

    def partition(b):
        return lax.rem(group + b, SIDE)

    def pool_copy(q):
        rows = pl.ds(q * (pool_ref.shape[0] // PIECES), pool_ref.shape[0] // PIECES)
        return pltpu.make_async_copy(pool_ref.at[rows], pool_buf.at[rows], pool_sem.at[q])

    small = [
        pltpu.make_async_copy(src, dst, small_sem.at[i])
        for i, (src, dst) in enumerate(
            [(assign_hbm, assign_ref), (sample_hbm, sample_ref), (counts_hbm, counts_ref), (old_hbm, old_ref)]
        )
    ]
    for copy in small:
        copy.start()
    for q in range(PIECES):
        pool_copy(q).start()
    own_inverse = pltpu.make_async_copy(precond_ref.at[group], inverse.at[0], own_sem)
    own_inverse.start()

    barrier = pltpu.get_barrier_semaphore()
    for a, b in FAR:
        pl.semaphore_signal(barrier, inc=1, device_id=(device(a, b), centre), device_id_type=MESH)
    for k in range(1, centre_count):
        pl.semaphore_signal(
            barrier, inc=1, device_id=(place, lax.rem(centre + k, centre_count)), device_id_type=MESH
        )

    first = centre * SIDE
    small[0].wait()
    assign = assign_ref[...]
    masks = [(assign == first + k) for k in range(SIDE)]
    mask_all = jnp.concatenate([m.astype(jnp.float32) for m in masks], axis=0).astype(jnp.bfloat16)
    lane_row, lane_col = iota((LANES, LANES), 0), iota((LANES, LANES), 1)
    upper = (lane_row <= lane_col).astype(jnp.float32).astype(jnp.bfloat16)
    inside = jnp.dot(mask_all, upper, preferred_element_type=jnp.float32)
    ones = jnp.ones((LANES, LANES), jnp.bfloat16)
    totals = jnp.dot(mask_all, ones, preferred_element_type=jnp.float32)
    span = assign.shape[0]
    big_row, big_col = iota((SIDE * span, SIDE * span), 0), iota((SIDE * span, SIDE * span), 1)
    same = (big_row // span) == (big_col // span)
    before = (same & (big_col < big_row)).astype(jnp.float32).astype(jnp.bfloat16)
    ahead = jnp.dot(before, totals.astype(jnp.bfloat16), preferred_element_type=jnp.float32)
    rank = (inside + ahead).astype(jnp.int32) - 1
    for k in range(SIDE):
        slot_of[k] = jnp.where(masks[k], rank[k * span : (k + 1) * span, :], -1)
    named = [jnp.sum(totals[k * span : (k + 1) * span, :], axis=0, keepdims=True) for k in range(SIDE)]

    small[1].wait()
    sample = sample_ref[...] + 1
    slot_row = iota((CAP, LANES), 0)
    times[...] = jnp.zeros(times.shape, jnp.float32)
    for k in range(SIDE):
        total = jnp.zeros((CAP, LANES), jnp.int32)
        for r in range(span):
            hit = slot_of[k, r : r + 1, :] == slot_row
            total += jnp.where(hit, sample[r : r + 1, :], 0)
        index = jnp.sum(total.astype(jnp.float32), axis=1, keepdims=True).astype(jnp.int32) - 1

        def pick(t, carry):
            hot = (iota((CAP, 256), 1) + t * 256) == index
            columns = pl.ds(pl.multiple_of(t * 256, 256), 256)
            hot = hot.astype(jnp.float32)
            picker[k * CAP : (k + 1) * CAP, columns] = hot.astype(jnp.bfloat16)
            times[k : k + 1, columns] = jnp.sum(hot, axis=0, keepdims=True)
            return carry

        lax.fori_loop(0, picker.shape[1] // 256, pick, 0, unroll=4)

    pl.semaphore_wait(barrier, SIDE * SIDE - 1 + centre_count - 1)
    inverse_copies = []
    for b in range(1, SIDE):
        copy = pltpu.make_async_remote_copy(
            src_ref=precond_ref.at[partition(b)],
            dst_ref=inverse.at[b],
            send_sem=inv_send.at[b],
            recv_sem=inv_recv.at[b],
            device_id=(device(0, b), centre),
            device_id_type=MESH,
        )
        copy.start()
        inverse_copies.append(copy)
    for q in range(PIECES):
        pool_copy(q).wait()
    tile_row = iota((CHUNKS, LANES), 0)
    half = lax.rem(place, 2)
    small[2].wait()
    small[3].wait()
    old = old_ref[...]
    sums = jnp.dot(times[...].astype(jnp.bfloat16), pool_buf[...], preferred_element_type=jnp.float32)
    twice = jnp.concatenate([old, old], axis=1)
    twice = jnp.where(iota(twice.shape, 1) // (LANES // 2) == half, twice, 0.0)
    for k in range(SIDE):
        rows = [sums[k : k + 1, r * LANES : (r + 1) * LANES] for r in range(CHUNKS)]
        tile = ANISO * jnp.concatenate(rows, axis=0)
        prior = counts_ref[k].astype(jnp.float32)
        tile += jnp.where(tile_row == place // 2, prior * twice[k : k + 1, :], 0.0)
        moment_out[k] = tile
        count_out[k] = jnp.broadcast_to(named[k], (CHUNKS, LANES))
    for a, b in FAR:
        pltpu.make_async_remote_copy(
            src_ref=moment_out.at[partition(b)],
            dst_ref=moment_in.at[a * SIDE + b],
            send_sem=moment_sem.at[0],
            recv_sem=moment_sem.at[1],
            device_id=(device(a, b), centre),
            device_id_type=MESH,
        ).start()

    row_copies = []
    for h in range(2):
        block = jnp.dot(picker[...], pool_buf[:, h * HALF : (h + 1) * HALF], preferred_element_type=jnp.float32)
        picked[h] = block.astype(jnp.bfloat16).reshape(SIDE, CAP, HALF)
        for b in range(1, SIDE):
            copy = pltpu.make_async_remote_copy(
                src_ref=picked.at[h, partition(b)],
                dst_ref=rows_in.at[h, b],
                send_sem=row_send.at[h, b],
                recv_sem=row_recv.at[h, b],
                device_id=(device(0, b), centre),
                device_id_type=MESH,
            )
            copy.start()
            row_copies.append(copy)
    count_copies = []
    for b in range(1, SIDE):
        copy = pltpu.make_async_remote_copy(
            src_ref=count_out.at[partition(b)],
            dst_ref=count_in.at[b],
            send_sem=count_send.at[b],
            recv_sem=count_recv.at[b],
            device_id=(device(0, b), centre),
            device_id_type=MESH,
        )
        copy.start()
        count_copies.append(copy)

    def piece(ref, part, rows, r):
        start = r % (CHUNKS // 2) * LANES
        return ref[r // (CHUNKS // 2), part, rows, start : start + LANES].astype(jnp.float32)

    def own_norm(k, carry):
        for i in range(CAP // 32):
            rows = slice(i * 32, (i + 1) * 32)
            total = jnp.zeros((32, LANES), jnp.float32)
            for r in range(CHUNKS):
                x = piece(picked, k, rows, r)
                total += x * x
            mean = jnp.sum(total, axis=1, keepdims=True) * (1.0 / D)
            inv_own[k, rows, :] = jnp.broadcast_to(lax.rsqrt(mean + EPSILON) / math.sqrt(D), (32, LANES))
        return carry

    lax.fori_loop(0, SIDE, own_norm, 0)

    own_inverse.wait()
    for copy in inverse_copies:
        copy.wait_recv()
    arrived = moment_in.at[pl.ds(1, SIDE * SIDE - 1)]
    pltpu.make_async_copy(arrived, arrived, moment_sem.at[1]).wait()
    moment = moment_out[group]
    for s in range(1, SIDE * SIDE):
        moment += moment_in[s]
    prior = counts_ref[group].astype(jnp.float32)
    scale = prior + mean_load
    moment = moment / scale

    block_row, block_lane = iota((64, LANES), 0), iota((64, LANES), 1)

    def apply_inverse(vector):
        tile = jnp.zeros((CHUNKS, LANES), jnp.float32)
        for b in range(SIDE):
            total = jnp.zeros((64, LANES), jnp.float32)
            for r in range(CHUNKS):
                w = inverse[b, :, r * LANES : (r + 1) * LANES].astype(jnp.float32)
                total += w * vector[r : r + 1, :]
            column = jnp.sum(total, axis=1, keepdims=True)
            home = device(0, SIDE - b)
            spread = jnp.where(block_lane == block_row + 64 * lax.rem(home, 2), column, 0.0)
            spread = jnp.sum(spread, axis=0, keepdims=True)
            tile += jnp.where(tile_row == home // 2, spread, 0.0)
        return tile

    def apply_outer(vector):
        alongs = []
        for i in range(SIDE * CAP // 32):
            total = jnp.zeros((32, LANES), jnp.float32)
            for r in range(CHUNKS):
                total += unit[i * 32 : (i + 1) * 32, r * LANES : (r + 1) * LANES] * vector[r : r + 1, :]
            alongs.append(jnp.sum(total, axis=1, keepdims=True))
        along = jnp.concatenate(alongs, axis=0)
        rows = []
        for r in range(CHUNKS):
            product = unit[:, r * LANES : (r + 1) * LANES] * along
            rows.append(jnp.sum(product, axis=0, keepdims=True))
        return jnp.concatenate(rows, axis=0)

    def line_sum(turn, tile):
        line_out[turn] = tile
        for a in (2, 1, 3):
            pltpu.make_async_remote_copy(
                src_ref=line_out.at[turn],
                dst_ref=line_in.at[turn, a],
                send_sem=line_send.at[turn],
                recv_sem=line_recv.at[turn],
                device_id=(device(a, 0), centre),
                device_id_type=MESH,
            ).start()
        here = line_in.at[turn, pl.ds(1, SIDE - 1)]

        def finish():
            pltpu.make_async_copy(here, here, line_recv.at[turn]).wait()
            return (tile + line_in[turn, 1]) + (line_in[turn, 2] + line_in[turn, 3])

        return finish

    finish = line_sum(0, apply_inverse(moment))

    for b in range(SIDE):
        if b:
            row_copies[b - 1].wait_recv()
            row_copies[b + SIDE - 2].wait_recv()

        for i in range(CAP // 32):
            rows = slice(i * 32, (i + 1) * 32)
            x = []
            for r in range(CHUNKS):
                x.append(piece(rows_in, b, rows, r) if b else piece(picked, group, rows, r))
            total = jnp.zeros((32, LANES), jnp.float32)
            for r in range(CHUNKS):
                total += x[r] * x[r]
            mean = jnp.sum(total, axis=1, keepdims=True) * (1.0 / D)
            inv = lax.rsqrt(mean + EPSILON) / math.sqrt(D)
            for r in range(CHUNKS):
                u = (x[r] * inv).astype(jnp.bfloat16).astype(jnp.float32)
                unit[b * CAP + i * 32 : b * CAP + (i + 1) * 32, r * LANES : (r + 1) * LANES] = u

    count = count_out[group]
    for b in range(1, SIDE):
        count_copies[b - 1].wait_recv()
        count += count_in[b]
    vector = finish()
    for sweep in range(SWEEPS):
        share = (ANISO - 1.0) * apply_outer(vector) + count * vector
        product = line_sum(2 * sweep + 1, share)()
        slack = moment - (product + prior * vector) / scale
        change = apply_inverse(slack)
        if sweep < SWEEPS - 1:
            vector = vector + line_sum(2 * sweep + 2, change)()

    lane = iota((CHUNKS, LANES), 1)
    mine = jnp.zeros((CHUNKS, LANES), jnp.float32)
    for b in range(SIDE):
        home = device(0, b)
        mine += jnp.where((tile_row == home // 2) & (lane // 64 == lax.rem(home, 2)), vector, 0.0)
    whole_out[...] = mine + change
    for a, b in FAR:
        pltpu.make_async_remote_copy(
            src_ref=whole_out,
            dst_ref=whole_in.at[a * SIDE + b],
            send_sem=whole_sem.at[0],
            recv_sem=whole_sem.at[1],
            device_id=(device(a, b), centre),
            device_id_type=MESH,
        ).start()
    arrived = whole_in.at[pl.ds(1, SIDE * SIDE - 1)]
    pltpu.make_async_copy(arrived, arrived, whole_sem.at[1]).wait()

    losses = jnp.zeros((span, LANES), jnp.float32)
    centres = jnp.zeros((SIDE, LANES), jnp.float32)
    part_row = iota((SIDE, LANES), 0)
    for b in range(SIDE):
        k = lax.rem(group + SIDE - b, SIDE)
        tile = whole_out[...] if b == 0 else whole_in[b]
        for a in range(1, SIDE):
            tile = tile + whole_in[a * SIDE + b]
        block = jnp.sum(jnp.where(tile_row == place // 2, tile, 0.0), axis=0, keepdims=True)
        centres += jnp.where(part_row == k, block, 0.0)

        columns = []
        for i in range(CAP // 32):
            rows = slice(i * 32, (i + 1) * 32)
            square = jnp.zeros((32, LANES), jnp.float32)
            along = jnp.zeros((32, LANES), jnp.float32)
            for r in range(CHUNKS):
                x = piece(picked, k, rows, r)
                deviation = x - tile[r : r + 1, :]
                square += deviation * deviation
                along += deviation * x
            along = jnp.sum(along, axis=1, keepdims=True) * inv_own[k, rows, 0:1]
            square = jnp.sum(square, axis=1, keepdims=True)
            columns.append((square + (ANISO - 1.0) * along * along) / (ANISO * D))
        column = jnp.concatenate(columns, axis=0)
        table = jnp.sum(jnp.where(lane_row == lane_col, column, 0.0), axis=0, keepdims=True)
        table = jnp.broadcast_to(table, (span, LANES))
        slots = slot_of[k]
        found = jnp.take_along_axis(table, jnp.maximum(slots, 0), axis=1)
        losses += jnp.where(slots >= 0, found, 0.0)

    loss_out[...] = losses
    for k in sorted(range(1, centre_count), key=lambda k: abs(2 * k - centre_count)):
        pltpu.make_async_remote_copy(
            src_ref=loss_out,
            dst_ref=loss_in.at[k],
            send_sem=loss_sem.at[0],
            recv_sem=loss_sem.at[1],
            device_id=(place, lax.rem(centre + k, centre_count)),
            device_id_type=MESH,
        ).start()

    swapped = jnp.concatenate([centres[:, 64:], centres[:, :64]], axis=1)
    centres_ref[...] = jnp.where(half == 0, centres, swapped)[:, :64]
    for copy in inverse_copies + row_copies + count_copies:
        copy.wait_send()
    sent = moment_in.at[pl.ds(1, SIDE * SIDE - 1)]
    pltpu.make_async_copy(sent, sent, moment_sem.at[0]).wait()
    for turn in range(2 * SWEEPS):
        sent = line_in.at[turn, pl.ds(1, SIDE - 1)]
        pltpu.make_async_copy(sent, sent, line_send.at[turn]).wait()
    sent = whole_in.at[pl.ds(1, SIDE * SIDE - 1)]
    pltpu.make_async_copy(sent, sent, whole_sem.at[0]).wait()
    if centre_count > 1:
        arrived = loss_in.at[pl.ds(1, centre_count - 1)]
        pltpu.make_async_copy(arrived, arrived, loss_sem.at[1]).wait()
        for k in range(1, centre_count):
            losses = losses + loss_in[k]
        pltpu.make_async_copy(arrived, arrived, loss_sem.at[0]).wait()
    loss_ref[...] = losses


def shards(pool, sample_idx, assign, counts, old_centres, precond):
    centre_count = lax.axis_size("centre")
    dp_count = lax.axis_size("dp")
    row_dev = sample_idx.shape[0]
    span = row_dev // LANES
    part_dev = counts.shape[0]
    mean_load = row_dev * dp_count / (part_dev * centre_count) * (D + ANISO - 1.0) / D
    pool_rows = pool.shape[0]
    f32, bf16 = jnp.float32, jnp.bfloat16
    vmem = pl.BlockSpec(memory_space=pltpu.VMEM)
    dma = pltpu.SemaphoreType.DMA
    plane = SIDE * SIDE
    centres, loss = pl.pallas_call(
        functools.partial(kernel, centre_count, mean_load),
        out_shape=(
            jax.ShapeDtypeStruct((part_dev, D // dp_count), f32),
            jax.ShapeDtypeStruct((span, LANES), f32),
        ),
        in_specs=[pl.BlockSpec(memory_space=pltpu.HBM)] * 6,
        out_specs=(vmem, vmem),
        scratch_shapes=[
            pltpu.VMEM((span, LANES), jnp.int32),
            pltpu.VMEM((span, LANES), jnp.int32),
            pltpu.SMEM((part_dev,), jnp.int32),
            pltpu.VMEM((part_dev, D // dp_count), f32),
            pltpu.VMEM((pool_rows, D), bf16),
            pltpu.VMEM((SIDE * CAP, pool_rows), bf16),
            pltpu.VMEM((8, pool_rows), f32),
            pltpu.VMEM((SIDE, span, LANES), jnp.int32),
            pltpu.VMEM((2, SIDE, CAP, HALF), bf16),
            pltpu.VMEM((2, SIDE, CAP, HALF), bf16),
            pltpu.VMEM((SIDE * CAP, D), f32),
            pltpu.VMEM((SIDE, CAP, LANES), f32),
            pltpu.VMEM((SIDE, D // dp_count, D), bf16),
            pltpu.VMEM((SIDE, CHUNKS, LANES), f32),
            pltpu.VMEM((plane, CHUNKS, LANES), f32),
            pltpu.VMEM((SIDE, CHUNKS, LANES), f32),
            pltpu.VMEM((SIDE, CHUNKS, LANES), f32),
            pltpu.VMEM((2 * SWEEPS, CHUNKS, LANES), f32),
            pltpu.VMEM((2 * SWEEPS, SIDE, CHUNKS, LANES), f32),
            pltpu.VMEM((CHUNKS, LANES), f32),
            pltpu.VMEM((plane, CHUNKS, LANES), f32),
            pltpu.VMEM((span, LANES), f32),
            pltpu.VMEM((centre_count, span, LANES), f32),
            dma((4,)),
            dma((PIECES,)),
            dma,
            dma((SIDE,)),
            dma((SIDE,)),
            dma((2, SIDE)),
            dma((2, SIDE)),
            dma((2,)),
            dma((SIDE,)),
            dma((SIDE,)),
            dma((2 * SWEEPS,)),
            dma((2 * SWEEPS,)),
            dma((2,)),
            dma((2,)),
        ],
        compiler_params=pltpu.CompilerParams(
            collective_id=0, has_side_effects=True, vmem_limit_bytes=48 * 1024 * 1024
        ),
    )(*(pltpu.with_memory_space_constraint(a, pltpu.HBM) for a in (sample_idx.reshape(span, LANES), assign.reshape(span, LANES), counts, old_centres, precond, pool)))
    return centres, loss.reshape(row_dev)


def solution(mesh):
    return jax.shard_map(
        shards,
        mesh=mesh,
        in_specs=(
            P("dp", None),
            P("dp"),
            P("dp"),
            P("centre"),
            P("centre", "dp"),
            P("centre", "dp", None),
        ),
        out_specs=(P("centre", "dp"), P("dp")),
        check_vma=False,
    )
```

```python
import functools
import math

import jax
import jax.numpy as jnp
from jax import lax
from jax.experimental import pallas as pl
from jax.experimental.pallas import tpu as pltpu
from jax.sharding import PartitionSpec as P

D = 1024
SWEEPS = 3
CAP = 128
THRESHOLD = 0.4
EPSILON = 1e-06
ANISO = (D - 1) * THRESHOLD**2 / (1 - THRESHOLD**2)

LANES = 128
CHUNKS = D // LANES
SIDE = 4
PIECES = 1
HALF = D // 2
MESH = pl.DeviceIdType.MESH


FAR = sorted(
    [(a, b) for a in range(SIDE) for b in range(SIDE) if a or b],
    key=lambda step: -sum(min(n, SIDE - n) for n in step),
)


def iota(shape, axis):
    return lax.broadcasted_iota(jnp.int32, shape, axis)


def kernel(
    centre_count,
    mean_load,
    sample_hbm,
    assign_hbm,
    counts_hbm,
    old_hbm,
    precond_ref,
    pool_ref,
    centres_ref,
    loss_ref,
    sample_ref,
    assign_ref,
    counts_ref,
    old_ref,
    pool_buf,
    picker,
    times,
    slot_of,
    picked,
    rows_in,
    unit,
    inv_own,
    inverse,
    moment_out,
    moment_in,
    count_out,
    count_in,
    line_out,
    line_in,
    whole_out,
    whole_in,
    loss_out,
    loss_in,
    small_sem,
    pool_sem,
    own_sem,
    inv_send,
    inv_recv,
    row_send,
    row_recv,
    moment_sem,
    count_send,
    count_recv,
    line_send,
    line_recv,
    whole_sem,
    loss_sem,
):
    place = lax.axis_index("dp")
    centre = lax.axis_index("centre")
    core = lax.rem(centre, 2)
    px, pz = place // SIDE, lax.rem(place, SIDE)
    group = (1 - core) * pz + core * px
    member = (1 - core) * px + core * pz

    def device(a, b):
        m, k = lax.rem(member + a, SIDE), lax.rem(group + b, SIDE)
        return (1 - core) * (m * SIDE + k) + core * (k * SIDE + m)

    def partition(b):
        return lax.rem(group + b, SIDE)

    def pool_copy(q):
        rows = pl.ds(q * (pool_ref.shape[0] // PIECES), pool_ref.shape[0] // PIECES)
        return pltpu.make_async_copy(pool_ref.at[rows], pool_buf.at[rows], pool_sem.at[q])

    small = [
        pltpu.make_async_copy(src, dst, small_sem.at[i])
        for i, (src, dst) in enumerate(
            [(assign_hbm, assign_ref), (sample_hbm, sample_ref), (counts_hbm, counts_ref), (old_hbm, old_ref)]
        )
    ]
    for copy in small:
        copy.start()
    for q in range(PIECES):
        pool_copy(q).start()
    own_inverse = pltpu.make_async_copy(precond_ref.at[group], inverse.at[0], own_sem)
    own_inverse.start()

    barrier = pltpu.get_barrier_semaphore()
    for a, b in FAR:
        pl.semaphore_signal(barrier, inc=1, device_id=(device(a, b), centre), device_id_type=MESH)
    for k in range(1, centre_count):
        pl.semaphore_signal(
            barrier, inc=1, device_id=(place, lax.rem(centre + k, centre_count)), device_id_type=MESH
        )

    first = centre * SIDE
    small[0].wait()
    assign = assign_ref[...]
    masks = [(assign == first + k) for k in range(SIDE)]
    mask_all = jnp.concatenate([m.astype(jnp.float32) for m in masks], axis=0).astype(jnp.bfloat16)
    lane_row, lane_col = iota((LANES, LANES), 0), iota((LANES, LANES), 1)
    upper = (lane_row <= lane_col).astype(jnp.float32).astype(jnp.bfloat16)
    inside = jnp.dot(mask_all, upper, preferred_element_type=jnp.float32)
    ones = jnp.ones((LANES, LANES), jnp.bfloat16)
    totals = jnp.dot(mask_all, ones, preferred_element_type=jnp.float32)
    span = assign.shape[0]
    big_row, big_col = iota((SIDE * span, SIDE * span), 0), iota((SIDE * span, SIDE * span), 1)
    same = (big_row // span) == (big_col // span)
    before = (same & (big_col < big_row)).astype(jnp.float32).astype(jnp.bfloat16)
    ahead = jnp.dot(before, totals.astype(jnp.bfloat16), preferred_element_type=jnp.float32)
    rank = (inside + ahead).astype(jnp.int32) - 1
    for k in range(SIDE):
        slot_of[k] = jnp.where(masks[k], rank[k * span : (k + 1) * span, :], -1)
    named = [jnp.sum(totals[k * span : (k + 1) * span, :], axis=0, keepdims=True) for k in range(SIDE)]

    small[1].wait()
    sample = sample_ref[...] + 1
    slot_row = iota((CAP, LANES), 0)
    times[...] = jnp.zeros(times.shape, jnp.float32)
    for k in range(SIDE):
        total = jnp.zeros((CAP, LANES), jnp.int32)
        for r in range(span):
            hit = slot_of[k, r : r + 1, :] == slot_row
            total += jnp.where(hit, sample[r : r + 1, :], 0)
        index = jnp.sum(total.astype(jnp.float32), axis=1, keepdims=True).astype(jnp.int32) - 1

        def pick(t, carry):
            hot = (iota((CAP, 256), 1) + t * 256) == index
            columns = pl.ds(pl.multiple_of(t * 256, 256), 256)
            hot = hot.astype(jnp.float32)
            picker[k * CAP : (k + 1) * CAP, columns] = hot.astype(jnp.bfloat16)
            times[k : k + 1, columns] = jnp.sum(hot, axis=0, keepdims=True)
            return carry

        lax.fori_loop(0, picker.shape[1] // 256, pick, 0, unroll=4)

    pl.semaphore_wait(barrier, SIDE * SIDE - 1 + centre_count - 1)
    inverse_copies = []
    for b in (2, 1, 3):
        copy = pltpu.make_async_remote_copy(
            src_ref=precond_ref.at[partition(b)],
            dst_ref=inverse.at[b],
            send_sem=inv_send.at[b],
            recv_sem=inv_recv.at[b],
            device_id=(device(0, b), centre),
            device_id_type=MESH,
        )
        copy.start()
        inverse_copies.append(copy)
    for q in range(PIECES):
        pool_copy(q).wait()
    tile_row = iota((CHUNKS, LANES), 0)
    half = lax.rem(place, 2)
    small[2].wait()
    small[3].wait()
    old = old_ref[...]
    sums = jnp.dot(times[...].astype(jnp.bfloat16), pool_buf[...], preferred_element_type=jnp.float32)
    twice = jnp.concatenate([old, old], axis=1)
    twice = jnp.where(iota(twice.shape, 1) // (LANES // 2) == half, twice, 0.0)
    for k in range(SIDE):
        rows = [sums[k : k + 1, r * LANES : (r + 1) * LANES] for r in range(CHUNKS)]
        tile = ANISO * jnp.concatenate(rows, axis=0)
        prior = counts_ref[k].astype(jnp.float32)
        tile += jnp.where(tile_row == place // 2, prior * twice[k : k + 1, :], 0.0)
        moment_out[k] = tile
        count_out[k] = jnp.broadcast_to(named[k], (CHUNKS, LANES))
    for a, b in FAR:
        pltpu.make_async_remote_copy(
            src_ref=moment_out.at[partition(b)],
            dst_ref=moment_in.at[a * SIDE + b],
            send_sem=moment_sem.at[0],
            recv_sem=moment_sem.at[1],
            device_id=(device(a, b), centre),
            device_id_type=MESH,
        ).start()

    row_copies = []
    for h in range(2):
        block = jnp.dot(picker[...], pool_buf[:, h * HALF : (h + 1) * HALF], preferred_element_type=jnp.float32)
        picked[h] = block.astype(jnp.bfloat16).reshape(SIDE, CAP, HALF)
        for b in range(1, SIDE):
            copy = pltpu.make_async_remote_copy(
                src_ref=picked.at[h, partition(b)],
                dst_ref=rows_in.at[h, b],
                send_sem=row_send.at[h, b],
                recv_sem=row_recv.at[h, b],
                device_id=(device(0, b), centre),
                device_id_type=MESH,
            )
            copy.start()
            row_copies.append(copy)
    count_copies = []
    for b in range(1, SIDE):
        copy = pltpu.make_async_remote_copy(
            src_ref=count_out.at[partition(b)],
            dst_ref=count_in.at[b],
            send_sem=count_send.at[b],
            recv_sem=count_recv.at[b],
            device_id=(device(0, b), centre),
            device_id_type=MESH,
        )
        copy.start()
        count_copies.append(copy)

    def piece(ref, part, rows, r):
        start = r % (CHUNKS // 2) * LANES
        return ref[r // (CHUNKS // 2), part, rows, start : start + LANES].astype(jnp.float32)

    def own_norm(k, carry):
        for i in range(CAP // 32):
            rows = slice(i * 32, (i + 1) * 32)
            total = jnp.zeros((32, LANES), jnp.float32)
            for r in range(CHUNKS):
                x = piece(picked, k, rows, r)
                total += x * x
            mean = jnp.sum(total, axis=1, keepdims=True) * (1.0 / D)
            inv_own[k, rows, :] = jnp.broadcast_to(lax.rsqrt(mean + EPSILON) / math.sqrt(D), (32, LANES))
        return carry

    own_inverse.wait()
    for copy in inverse_copies:
        copy.wait_recv()
    arrived = moment_in.at[pl.ds(1, SIDE * SIDE - 1)]
    pltpu.make_async_copy(arrived, arrived, moment_sem.at[1]).wait()
    moment = moment_out[group]
    for s in range(1, SIDE * SIDE):
        moment += moment_in[s]
    prior = counts_ref[group].astype(jnp.float32)
    scale = prior + mean_load
    moment = moment / scale

    block_row, block_lane = iota((64, LANES), 0), iota((64, LANES), 1)

    def apply_inverse(vector):
        tile = jnp.zeros((CHUNKS, LANES), jnp.float32)
        for b in range(SIDE):
            total = jnp.zeros((64, LANES), jnp.float32)
            for r in range(CHUNKS):
                w = inverse[b, :, r * LANES : (r + 1) * LANES].astype(jnp.float32)
                total += w * vector[r : r + 1, :]
            column = jnp.sum(total, axis=1, keepdims=True)
            home = device(0, SIDE - b)
            spread = jnp.where(block_lane == block_row + 64 * lax.rem(home, 2), column, 0.0)
            spread = jnp.sum(spread, axis=0, keepdims=True)
            tile += jnp.where(tile_row == home // 2, spread, 0.0)
        return tile

    def apply_outer(vector):
        alongs = []
        for i in range(SIDE * CAP // 32):
            total = jnp.zeros((32, LANES), jnp.float32)
            for r in range(CHUNKS):
                total += unit[i * 32 : (i + 1) * 32, r * LANES : (r + 1) * LANES] * vector[r : r + 1, :]
            alongs.append(jnp.sum(total, axis=1, keepdims=True))
        along = jnp.concatenate(alongs, axis=0)
        rows = []
        for r in range(CHUNKS):
            product = unit[:, r * LANES : (r + 1) * LANES] * along
            rows.append(jnp.sum(product, axis=0, keepdims=True))
        return jnp.concatenate(rows, axis=0)

    def line_sum(turn, tile):
        line_out[turn] = tile
        for a in (2, 1, 3):
            pltpu.make_async_remote_copy(
                src_ref=line_out.at[turn],
                dst_ref=line_in.at[turn, a],
                send_sem=line_send.at[turn],
                recv_sem=line_recv.at[turn],
                device_id=(device(a, 0), centre),
                device_id_type=MESH,
            ).start()
        here = line_in.at[turn, pl.ds(1, SIDE - 1)]

        def finish():
            pltpu.make_async_copy(here, here, line_recv.at[turn]).wait()
            return (tile + line_in[turn, 1]) + (line_in[turn, 2] + line_in[turn, 3])

        return finish

    finish = line_sum(0, apply_inverse(moment))

    for b in range(SIDE):
        if b:
            row_copies[b - 1].wait_recv()
            row_copies[b + SIDE - 2].wait_recv()

        for i in range(CAP // 32):
            rows = slice(i * 32, (i + 1) * 32)
            x = []
            for r in range(CHUNKS):
                x.append(piece(rows_in, b, rows, r) if b else piece(picked, group, rows, r))
            total = jnp.zeros((32, LANES), jnp.float32)
            for r in range(CHUNKS):
                total += x[r] * x[r]
            mean = jnp.sum(total, axis=1, keepdims=True) * (1.0 / D)
            inv = lax.rsqrt(mean + EPSILON) / math.sqrt(D)
            for r in range(CHUNKS):
                u = (x[r] * inv).astype(jnp.bfloat16).astype(jnp.float32)
                unit[b * CAP + i * 32 : b * CAP + (i + 1) * 32, r * LANES : (r + 1) * LANES] = u

    count = count_out[group]
    for b in range(1, SIDE):
        count_copies[b - 1].wait_recv()
        count += count_in[b]
    vector = finish()
    for sweep in range(SWEEPS):
        share = (ANISO - 1.0) * apply_outer(vector) + count * vector
        finish = line_sum(2 * sweep + 1, share)
        if sweep == 0:
            lax.fori_loop(0, SIDE, own_norm, 0)
        product = finish()
        slack = moment - (product + prior * vector) / scale
        change = apply_inverse(slack)
        if sweep < SWEEPS - 1:
            vector = vector + line_sum(2 * sweep + 2, change)()

    lane = iota((CHUNKS, LANES), 1)
    mine = jnp.zeros((CHUNKS, LANES), jnp.float32)
    for b in range(SIDE):
        home = device(0, b)
        mine += jnp.where((tile_row == home // 2) & (lane // 64 == lax.rem(home, 2)), vector, 0.0)
    whole_out[...] = mine + change
    for a, b in FAR:
        pltpu.make_async_remote_copy(
            src_ref=whole_out,
            dst_ref=whole_in.at[a * SIDE + b],
            send_sem=whole_sem.at[0],
            recv_sem=whole_sem.at[1],
            device_id=(device(a, b), centre),
            device_id_type=MESH,
        ).start()
    arrived = whole_in.at[pl.ds(1, SIDE * SIDE - 1)]
    pltpu.make_async_copy(arrived, arrived, whole_sem.at[1]).wait()

    losses = jnp.zeros((span, LANES), jnp.float32)
    centres = jnp.zeros((SIDE, LANES), jnp.float32)
    part_row = iota((SIDE, LANES), 0)
    for b in range(SIDE):
        k = lax.rem(group + SIDE - b, SIDE)
        tile = whole_out[...] if b == 0 else whole_in[b]
        for a in range(1, SIDE):
            tile = tile + whole_in[a * SIDE + b]
        block = jnp.sum(jnp.where(tile_row == place // 2, tile, 0.0), axis=0, keepdims=True)
        centres += jnp.where(part_row == k, block, 0.0)

        columns = []
        for i in range(CAP // 32):
            rows = slice(i * 32, (i + 1) * 32)
            square = jnp.zeros((32, LANES), jnp.float32)
            along = jnp.zeros((32, LANES), jnp.float32)
            for r in range(CHUNKS):
                x = piece(picked, k, rows, r)
                deviation = x - tile[r : r + 1, :]
                square += deviation * deviation
                along += deviation * x
            along = jnp.sum(along, axis=1, keepdims=True) * inv_own[k, rows, 0:1]
            square = jnp.sum(square, axis=1, keepdims=True)
            columns.append((square + (ANISO - 1.0) * along * along) / (ANISO * D))
        column = jnp.concatenate(columns, axis=0)
        table = jnp.sum(jnp.where(lane_row == lane_col, column, 0.0), axis=0, keepdims=True)
        table = jnp.broadcast_to(table, (span, LANES))
        slots = slot_of[k]
        found = jnp.take_along_axis(table, jnp.maximum(slots, 0), axis=1)
        losses += jnp.where(slots >= 0, found, 0.0)

    loss_out[...] = losses
    for k in sorted(range(1, centre_count), key=lambda k: abs(2 * k - centre_count)):
        pltpu.make_async_remote_copy(
            src_ref=loss_out,
            dst_ref=loss_in.at[k],
            send_sem=loss_sem.at[0],
            recv_sem=loss_sem.at[1],
            device_id=(place, lax.rem(centre + k, centre_count)),
            device_id_type=MESH,
        ).start()

    swapped = jnp.concatenate([centres[:, 64:], centres[:, :64]], axis=1)
    centres_ref[...] = jnp.where(half == 0, centres, swapped)[:, :64]
    for copy in inverse_copies + row_copies + count_copies:
        copy.wait_send()
    sent = moment_in.at[pl.ds(1, SIDE * SIDE - 1)]
    pltpu.make_async_copy(sent, sent, moment_sem.at[0]).wait()
    for turn in range(2 * SWEEPS):
        sent = line_in.at[turn, pl.ds(1, SIDE - 1)]
        pltpu.make_async_copy(sent, sent, line_send.at[turn]).wait()
    sent = whole_in.at[pl.ds(1, SIDE * SIDE - 1)]
    pltpu.make_async_copy(sent, sent, whole_sem.at[0]).wait()
    if centre_count > 1:
        arrived = loss_in.at[pl.ds(1, centre_count - 1)]
        pltpu.make_async_copy(arrived, arrived, loss_sem.at[1]).wait()
        for k in range(1, centre_count):
            losses = losses + loss_in[k]
        pltpu.make_async_copy(arrived, arrived, loss_sem.at[0]).wait()
    loss_ref[...] = losses


def shards(pool, sample_idx, assign, counts, old_centres, precond):
    centre_count = lax.axis_size("centre")
    dp_count = lax.axis_size("dp")
    row_dev = sample_idx.shape[0]
    span = row_dev // LANES
    part_dev = counts.shape[0]
    mean_load = row_dev * dp_count / (part_dev * centre_count) * (D + ANISO - 1.0) / D
    pool_rows = pool.shape[0]
    f32, bf16 = jnp.float32, jnp.bfloat16
    vmem = pl.BlockSpec(memory_space=pltpu.VMEM)
    dma = pltpu.SemaphoreType.DMA
    plane = SIDE * SIDE
    centres, loss = pl.pallas_call(
        functools.partial(kernel, centre_count, mean_load),
        out_shape=(
            jax.ShapeDtypeStruct((part_dev, D // dp_count), f32),
            jax.ShapeDtypeStruct((span, LANES), f32),
        ),
        in_specs=[pl.BlockSpec(memory_space=pltpu.HBM)] * 6,
        out_specs=(vmem, vmem),
        scratch_shapes=[
            pltpu.VMEM((span, LANES), jnp.int32),
            pltpu.VMEM((span, LANES), jnp.int32),
            pltpu.SMEM((part_dev,), jnp.int32),
            pltpu.VMEM((part_dev, D // dp_count), f32),
            pltpu.VMEM((pool_rows, D), bf16),
            pltpu.VMEM((SIDE * CAP, pool_rows), bf16),
            pltpu.VMEM((8, pool_rows), f32),
            pltpu.VMEM((SIDE, span, LANES), jnp.int32),
            pltpu.VMEM((2, SIDE, CAP, HALF), bf16),
            pltpu.VMEM((2, SIDE, CAP, HALF), bf16),
            pltpu.VMEM((SIDE * CAP, D), f32),
            pltpu.VMEM((SIDE, CAP, LANES), f32),
            pltpu.VMEM((SIDE, D // dp_count, D), bf16),
            pltpu.VMEM((SIDE, CHUNKS, LANES), f32),
            pltpu.VMEM((plane, CHUNKS, LANES), f32),
            pltpu.VMEM((SIDE, CHUNKS, LANES), f32),
            pltpu.VMEM((SIDE, CHUNKS, LANES), f32),
            pltpu.VMEM((2 * SWEEPS, CHUNKS, LANES), f32),
            pltpu.VMEM((2 * SWEEPS, SIDE, CHUNKS, LANES), f32),
            pltpu.VMEM((CHUNKS, LANES), f32),
            pltpu.VMEM((plane, CHUNKS, LANES), f32),
            pltpu.VMEM((span, LANES), f32),
            pltpu.VMEM((centre_count, span, LANES), f32),
            dma((4,)),
            dma((PIECES,)),
            dma,
            dma((SIDE,)),
            dma((SIDE,)),
            dma((2, SIDE)),
            dma((2, SIDE)),
            dma((2,)),
            dma((SIDE,)),
            dma((SIDE,)),
            dma((2 * SWEEPS,)),
            dma((2 * SWEEPS,)),
            dma((2,)),
            dma((2,)),
        ],
        compiler_params=pltpu.CompilerParams(
            collective_id=0, has_side_effects=True, vmem_limit_bytes=48 * 1024 * 1024
        ),
    )(*(pltpu.with_memory_space_constraint(a, pltpu.HBM) for a in (sample_idx.reshape(span, LANES), assign.reshape(span, LANES), counts, old_centres, precond, pool)))
    return centres, loss.reshape(row_dev)


def solution(mesh):
    return jax.shard_map(
        shards,
        mesh=mesh,
        in_specs=(
            P("dp", None),
            P("dp"),
            P("dp"),
            P("centre"),
            P("centre", "dp"),
            P("centre", "dp", None),
        ),
        out_specs=(P("centre", "dp"), P("dp")),
        check_vma=False,
    )
```

```python
import functools
import math

import jax
import jax.numpy as jnp
from jax import lax
from jax.experimental import pallas as pl
from jax.experimental.pallas import tpu as pltpu
from jax.sharding import PartitionSpec as P

D = 1024
SWEEPS = 3
CAP = 128
THRESHOLD = 0.4
EPSILON = 1e-06
ANISO = (D - 1) * THRESHOLD**2 / (1 - THRESHOLD**2)

LANES = 128
CHUNKS = D // LANES
SIDE = 4
PIECES = 1
HALF = D // 2
MESH = pl.DeviceIdType.MESH


FAR = sorted(
    [(a, b) for a in range(SIDE) for b in range(SIDE) if a or b],
    key=lambda step: -sum(min(n, SIDE - n) for n in step),
)


def iota(shape, axis):
    return lax.broadcasted_iota(jnp.int32, shape, axis)


def kernel(
    centre_count,
    mean_load,
    sample_hbm,
    assign_hbm,
    counts_hbm,
    old_hbm,
    precond_ref,
    pool_ref,
    centres_ref,
    loss_ref,
    sample_ref,
    assign_ref,
    counts_ref,
    old_ref,
    pool_buf,
    picker,
    times,
    slot_of,
    picked,
    rows_in,
    unit,
    inv_own,
    inverse,
    moment_out,
    moment_in,
    count_out,
    count_in,
    line_out,
    line_in,
    whole_out,
    whole_in,
    loss_out,
    loss_in,
    small_sem,
    pool_sem,
    own_sem,
    inv_send,
    inv_recv,
    row_send,
    row_recv,
    moment_sem,
    count_send,
    count_recv,
    line_send,
    line_recv,
    whole_sem,
    loss_sem,
):
    place = lax.axis_index("dp")
    centre = lax.axis_index("centre")
    core = lax.rem(centre, 2)
    px, pz = place // SIDE, lax.rem(place, SIDE)
    group = (1 - core) * pz + core * px
    member = (1 - core) * px + core * pz

    def device(a, b):
        m, k = lax.rem(member + a, SIDE), lax.rem(group + b, SIDE)
        return (1 - core) * (m * SIDE + k) + core * (k * SIDE + m)

    def partition(b):
        return lax.rem(group + b, SIDE)

    def pool_copy(q):
        rows = pl.ds(q * (pool_ref.shape[0] // PIECES), pool_ref.shape[0] // PIECES)
        return pltpu.make_async_copy(pool_ref.at[rows], pool_buf.at[rows], pool_sem.at[q])

    small = [
        pltpu.make_async_copy(src, dst, small_sem.at[i])
        for i, (src, dst) in enumerate(
            [(assign_hbm, assign_ref), (sample_hbm, sample_ref), (counts_hbm, counts_ref), (old_hbm, old_ref)]
        )
    ]
    for copy in small:
        copy.start()
    for q in range(PIECES):
        pool_copy(q).start()
    own_inverse = pltpu.make_async_copy(precond_ref.at[group], inverse.at[0], own_sem)
    own_inverse.start()

    barrier = pltpu.get_barrier_semaphore()
    for a, b in FAR:
        pl.semaphore_signal(barrier, inc=1, device_id=(device(a, b), centre), device_id_type=MESH)
    for k in range(1, centre_count):
        pl.semaphore_signal(
            barrier, inc=1, device_id=(place, lax.rem(centre + k, centre_count)), device_id_type=MESH
        )

    first = centre * SIDE
    small[0].wait()
    assign = assign_ref[...]
    masks = [(assign == first + k) for k in range(SIDE)]
    mask_all = jnp.concatenate([m.astype(jnp.float32) for m in masks], axis=0).astype(jnp.bfloat16)
    lane_row, lane_col = iota((LANES, LANES), 0), iota((LANES, LANES), 1)
    upper = (lane_row <= lane_col).astype(jnp.float32).astype(jnp.bfloat16)
    inside = jnp.dot(mask_all, upper, preferred_element_type=jnp.float32)
    ones = jnp.ones((LANES, LANES), jnp.bfloat16)
    totals = jnp.dot(mask_all, ones, preferred_element_type=jnp.float32)
    span = assign.shape[0]
    big_row, big_col = iota((SIDE * span, SIDE * span), 0), iota((SIDE * span, SIDE * span), 1)
    same = (big_row // span) == (big_col // span)
    before = (same & (big_col < big_row)).astype(jnp.float32).astype(jnp.bfloat16)
    ahead = jnp.dot(before, totals.astype(jnp.bfloat16), preferred_element_type=jnp.float32)
    rank = (inside + ahead).astype(jnp.int32) - 1
    for k in range(SIDE):
        slot_of[k] = jnp.where(masks[k], rank[k * span : (k + 1) * span, :], -1)
    named = [jnp.sum(totals[k * span : (k + 1) * span, :], axis=0, keepdims=True) for k in range(SIDE)]

    small[1].wait()
    sample = (sample_ref[...] + 1).astype(jnp.float32)
    slot_row = iota((CAP, LANES), 0)
    times[...] = jnp.zeros(times.shape, jnp.float32)
    indices = []
    for k in range(SIDE):
        total = jnp.zeros((CAP, LANES), jnp.float32)
        for r in range(span):
            hit = slot_of[k, r : r + 1, :] == slot_row
            total += jnp.where(hit, sample[r : r + 1, :], 0.0)
        indices.append(jnp.sum(total, axis=1, keepdims=True).astype(jnp.int32) - 1)

    def pick(t, carry):
        columns = pl.ds(pl.multiple_of(t * 256, 256), 256)
        ident = iota((CAP, 256), 1) + t * 256
        for k in range(SIDE):
            hot = (ident == indices[k]).astype(jnp.float32)
            picker[k * CAP : (k + 1) * CAP, columns] = hot.astype(jnp.bfloat16)
            times[k : k + 1, columns] = jnp.sum(hot, axis=0, keepdims=True)
        return carry

    lax.fori_loop(0, picker.shape[1] // 256, pick, 0, unroll=1)

    pl.semaphore_wait(barrier, SIDE * SIDE - 1 + centre_count - 1)
    inverse_copies = []
    for b in (2, 1, 3):
        copy = pltpu.make_async_remote_copy(
            src_ref=precond_ref.at[partition(b)],
            dst_ref=inverse.at[b],
            send_sem=inv_send.at[b],
            recv_sem=inv_recv.at[b],
            device_id=(device(0, b), centre),
            device_id_type=MESH,
        )
        copy.start()
        inverse_copies.append(copy)
    for q in range(PIECES):
        pool_copy(q).wait()
    tile_row = iota((CHUNKS, LANES), 0)
    half = lax.rem(place, 2)
    small[2].wait()
    small[3].wait()
    old = old_ref[...]
    sums = jnp.dot(times[...].astype(jnp.bfloat16), pool_buf[...], preferred_element_type=jnp.float32)
    twice = jnp.concatenate([old, old], axis=1)
    twice = jnp.where(iota(twice.shape, 1) // (LANES // 2) == half, twice, 0.0)
    for k in range(SIDE):
        rows = [sums[k : k + 1, r * LANES : (r + 1) * LANES] for r in range(CHUNKS)]
        tile = ANISO * jnp.concatenate(rows, axis=0)
        prior = counts_ref[k].astype(jnp.float32)
        tile += jnp.where(tile_row == place // 2, prior * twice[k : k + 1, :], 0.0)
        moment_out[k] = tile
        count_out[k] = jnp.broadcast_to(named[k], (CHUNKS, LANES))
    for a, b in FAR:
        pltpu.make_async_remote_copy(
            src_ref=moment_out.at[partition(b)],
            dst_ref=moment_in.at[a * SIDE + b],
            send_sem=moment_sem.at[0],
            recv_sem=moment_sem.at[1],
            device_id=(device(a, b), centre),
            device_id_type=MESH,
        ).start()

    row_copies = []
    for h in range(2):
        block = jnp.dot(picker[...], pool_buf[:, h * HALF : (h + 1) * HALF], preferred_element_type=jnp.float32)
        picked[h] = block.astype(jnp.bfloat16).reshape(SIDE, CAP, HALF)
        for b in range(1, SIDE):
            copy = pltpu.make_async_remote_copy(
                src_ref=picked.at[h, partition(b)],
                dst_ref=rows_in.at[h, b],
                send_sem=row_send.at[h, b],
                recv_sem=row_recv.at[h, b],
                device_id=(device(0, b), centre),
                device_id_type=MESH,
            )
            copy.start()
            row_copies.append(copy)
    count_copies = []
    for b in range(1, SIDE):
        copy = pltpu.make_async_remote_copy(
            src_ref=count_out.at[partition(b)],
            dst_ref=count_in.at[b],
            send_sem=count_send.at[b],
            recv_sem=count_recv.at[b],
            device_id=(device(0, b), centre),
            device_id_type=MESH,
        )
        copy.start()
        count_copies.append(copy)

    def piece(ref, part, rows, r):
        start = r % (CHUNKS // 2) * LANES
        return ref[r // (CHUNKS // 2), part, rows, start : start + LANES].astype(jnp.float32)

    def own_norm(k, carry):
        for i in range(CAP // 32):
            rows = slice(i * 32, (i + 1) * 32)
            total = jnp.zeros((32, LANES), jnp.float32)
            for r in range(CHUNKS):
                x = piece(picked, k, rows, r)
                total += x * x
            mean = jnp.sum(total, axis=1, keepdims=True) * (1.0 / D)
            inv_own[k, rows, :] = jnp.broadcast_to(lax.rsqrt(mean + EPSILON) / math.sqrt(D), (32, LANES))
        return carry

    own_inverse.wait()
    for copy in inverse_copies:
        copy.wait_recv()
    arrived = moment_in.at[pl.ds(1, SIDE * SIDE - 1)]
    pltpu.make_async_copy(arrived, arrived, moment_sem.at[1]).wait()
    moment = moment_out[group]
    for s in range(1, SIDE * SIDE):
        moment += moment_in[s]
    prior = counts_ref[group].astype(jnp.float32)
    scale = prior + mean_load
    moment = moment / scale

    block_row, block_lane = iota((64, LANES), 0), iota((64, LANES), 1)

    def apply_inverse(vector):
        tile = jnp.zeros((CHUNKS, LANES), jnp.float32)
        for b in range(SIDE):
            total = jnp.zeros((64, LANES), jnp.float32)
            for r in range(CHUNKS):
                w = inverse[b, :, r * LANES : (r + 1) * LANES].astype(jnp.float32)
                total += w * vector[r : r + 1, :]
            column = jnp.sum(total, axis=1, keepdims=True)
            home = device(0, SIDE - b)
            spread = jnp.where(block_lane == block_row + 64 * lax.rem(home, 2), column, 0.0)
            spread = jnp.sum(spread, axis=0, keepdims=True)
            tile += jnp.where(tile_row == home // 2, spread, 0.0)
        return tile

    def apply_outer(vector):
        parts = [jnp.zeros((8, LANES), jnp.float32) for _ in range(CHUNKS)]
        for i in range(SIDE * CAP // 32):
            total = jnp.zeros((32, LANES), jnp.float32)
            pieces = []
            for r in range(CHUNKS):
                u = unit[i * 32 : (i + 1) * 32, r * LANES : (r + 1) * LANES]
                pieces.append(u)
                total += u * vector[r : r + 1, :]
            along = jnp.sum(total, axis=1, keepdims=True)
            for r in range(CHUNKS):
                v = pieces[r] * along
                parts[r] += (v[0:8] + v[8:16]) + (v[16:24] + v[24:32])
        return jnp.concatenate([jnp.sum(p, axis=0, keepdims=True) for p in parts], axis=0)

    def line_sum(turn, tile):
        line_out[turn] = tile
        for a in (2, 1, 3):
            pltpu.make_async_remote_copy(
                src_ref=line_out.at[turn],
                dst_ref=line_in.at[turn, a],
                send_sem=line_send.at[turn],
                recv_sem=line_recv.at[turn],
                device_id=(device(a, 0), centre),
                device_id_type=MESH,
            ).start()
        here = line_in.at[turn, pl.ds(1, SIDE - 1)]

        def finish():
            pltpu.make_async_copy(here, here, line_recv.at[turn]).wait()
            return (tile + line_in[turn, 1]) + (line_in[turn, 2] + line_in[turn, 3])

        return finish

    finish = line_sum(0, apply_inverse(moment))

    for b in range(SIDE):
        if b:
            row_copies[b - 1].wait_recv()
            row_copies[b + SIDE - 2].wait_recv()

        for i in range(CAP // 32):
            rows = slice(i * 32, (i + 1) * 32)
            x = []
            for r in range(CHUNKS):
                x.append(piece(rows_in, b, rows, r) if b else piece(picked, group, rows, r))
            total = jnp.zeros((32, LANES), jnp.float32)
            for r in range(CHUNKS):
                total += x[r] * x[r]
            mean = jnp.sum(total, axis=1, keepdims=True) * (1.0 / D)
            inv = lax.rsqrt(mean + EPSILON) / math.sqrt(D)
            for r in range(CHUNKS):
                u = (x[r] * inv).astype(jnp.bfloat16).astype(jnp.float32)
                unit[b * CAP + i * 32 : b * CAP + (i + 1) * 32, r * LANES : (r + 1) * LANES] = u

    count = count_out[group]
    for b in range(1, SIDE):
        count_copies[b - 1].wait_recv()
        count += count_in[b]
    vector = finish()
    for sweep in range(SWEEPS):
        share = (ANISO - 1.0) * apply_outer(vector) + count * vector
        finish = line_sum(2 * sweep + 1, share)
        if sweep == 0:
            lax.fori_loop(0, SIDE, own_norm, 0)
        product = finish()
        slack = moment - (product + prior * vector) / scale
        change = apply_inverse(slack)
        if sweep < SWEEPS - 1:
            vector = vector + line_sum(2 * sweep + 2, change)()

    lane = iota((CHUNKS, LANES), 1)
    mine = jnp.zeros((CHUNKS, LANES), jnp.float32)
    for b in range(SIDE):
        home = device(0, b)
        mine += jnp.where((tile_row == home // 2) & (lane // 64 == lax.rem(home, 2)), vector, 0.0)
    whole_out[...] = mine + change
    for a, b in FAR:
        pltpu.make_async_remote_copy(
            src_ref=whole_out,
            dst_ref=whole_in.at[a * SIDE + b],
            send_sem=whole_sem.at[0],
            recv_sem=whole_sem.at[1],
            device_id=(device(a, b), centre),
            device_id_type=MESH,
        ).start()
    arrived = whole_in.at[pl.ds(1, SIDE * SIDE - 1)]
    pltpu.make_async_copy(arrived, arrived, whole_sem.at[1]).wait()

    losses = jnp.zeros((span, LANES), jnp.float32)
    centres = jnp.zeros((SIDE, LANES), jnp.float32)
    part_row = iota((SIDE, LANES), 0)
    for b in range(SIDE):
        k = lax.rem(group + SIDE - b, SIDE)
        tile = whole_out[...] if b == 0 else whole_in[b]
        for a in range(1, SIDE):
            tile = tile + whole_in[a * SIDE + b]
        block = jnp.sum(jnp.where(tile_row == place // 2, tile, 0.0), axis=0, keepdims=True)
        centres += jnp.where(part_row == k, block, 0.0)

        columns = []
        for i in range(CAP // 32):
            rows = slice(i * 32, (i + 1) * 32)
            square = jnp.zeros((32, LANES), jnp.float32)
            along = jnp.zeros((32, LANES), jnp.float32)
            for r in range(CHUNKS):
                x = piece(picked, k, rows, r)
                deviation = x - tile[r : r + 1, :]
                square += deviation * deviation
                along += deviation * x
            along = jnp.sum(along, axis=1, keepdims=True) * inv_own[k, rows, 0:1]
            square = jnp.sum(square, axis=1, keepdims=True)
            columns.append((square + (ANISO - 1.0) * along * along) / (ANISO * D))
        column = jnp.concatenate(columns, axis=0)
        table = jnp.sum(jnp.where(lane_row == lane_col, column, 0.0), axis=0, keepdims=True)
        table = jnp.broadcast_to(table, (span, LANES))
        slots = slot_of[k]
        found = jnp.take_along_axis(table, jnp.maximum(slots, 0), axis=1)
        losses += jnp.where(slots >= 0, found, 0.0)

    loss_out[...] = losses
    for k in sorted(range(1, centre_count), key=lambda k: abs(2 * k - centre_count)):
        pltpu.make_async_remote_copy(
            src_ref=loss_out,
            dst_ref=loss_in.at[k],
            send_sem=loss_sem.at[0],
            recv_sem=loss_sem.at[1],
            device_id=(place, lax.rem(centre + k, centre_count)),
            device_id_type=MESH,
        ).start()

    swapped = jnp.concatenate([centres[:, 64:], centres[:, :64]], axis=1)
    centres_ref[...] = jnp.where(half == 0, centres, swapped)[:, :64]
    for copy in inverse_copies + row_copies + count_copies:
        copy.wait_send()
    sent = moment_in.at[pl.ds(1, SIDE * SIDE - 1)]
    pltpu.make_async_copy(sent, sent, moment_sem.at[0]).wait()
    for turn in range(2 * SWEEPS):
        sent = line_in.at[turn, pl.ds(1, SIDE - 1)]
        pltpu.make_async_copy(sent, sent, line_send.at[turn]).wait()
    sent = whole_in.at[pl.ds(1, SIDE * SIDE - 1)]
    pltpu.make_async_copy(sent, sent, whole_sem.at[0]).wait()
    if centre_count > 1:
        arrived = loss_in.at[pl.ds(1, centre_count - 1)]
        pltpu.make_async_copy(arrived, arrived, loss_sem.at[1]).wait()
        for k in range(1, centre_count):
            losses = losses + loss_in[k]
        pltpu.make_async_copy(arrived, arrived, loss_sem.at[0]).wait()
    loss_ref[...] = losses


def shards(pool, sample_idx, assign, counts, old_centres, precond):
    centre_count = lax.axis_size("centre")
    dp_count = lax.axis_size("dp")
    row_dev = sample_idx.shape[0]
    span = row_dev // LANES
    part_dev = counts.shape[0]
    mean_load = row_dev * dp_count / (part_dev * centre_count) * (D + ANISO - 1.0) / D
    pool_rows = pool.shape[0]
    f32, bf16 = jnp.float32, jnp.bfloat16
    vmem = pl.BlockSpec(memory_space=pltpu.VMEM)
    dma = pltpu.SemaphoreType.DMA
    plane = SIDE * SIDE
    centres, loss = pl.pallas_call(
        functools.partial(kernel, centre_count, mean_load),
        out_shape=(
            jax.ShapeDtypeStruct((part_dev, D // dp_count), f32),
            jax.ShapeDtypeStruct((span, LANES), f32),
        ),
        in_specs=[pl.BlockSpec(memory_space=pltpu.HBM)] * 6,
        out_specs=(vmem, vmem),
        scratch_shapes=[
            pltpu.VMEM((span, LANES), jnp.int32),
            pltpu.VMEM((span, LANES), jnp.int32),
            pltpu.SMEM((part_dev,), jnp.int32),
            pltpu.VMEM((part_dev, D // dp_count), f32),
            pltpu.VMEM((pool_rows, D), bf16),
            pltpu.VMEM((SIDE * CAP, pool_rows), bf16),
            pltpu.VMEM((8, pool_rows), f32),
            pltpu.VMEM((SIDE, span, LANES), jnp.int32),
            pltpu.VMEM((2, SIDE, CAP, HALF), bf16),
            pltpu.VMEM((2, SIDE, CAP, HALF), bf16),
            pltpu.VMEM((SIDE * CAP, D), f32),
            pltpu.VMEM((SIDE, CAP, LANES), f32),
            pltpu.VMEM((SIDE, D // dp_count, D), bf16),
            pltpu.VMEM((SIDE, CHUNKS, LANES), f32),
            pltpu.VMEM((plane, CHUNKS, LANES), f32),
            pltpu.VMEM((SIDE, CHUNKS, LANES), f32),
            pltpu.VMEM((SIDE, CHUNKS, LANES), f32),
            pltpu.VMEM((2 * SWEEPS, CHUNKS, LANES), f32),
            pltpu.VMEM((2 * SWEEPS, SIDE, CHUNKS, LANES), f32),
            pltpu.VMEM((CHUNKS, LANES), f32),
            pltpu.VMEM((plane, CHUNKS, LANES), f32),
            pltpu.VMEM((span, LANES), f32),
            pltpu.VMEM((centre_count, span, LANES), f32),
            dma((4,)),
            dma((PIECES,)),
            dma,
            dma((SIDE,)),
            dma((SIDE,)),
            dma((2, SIDE)),
            dma((2, SIDE)),
            dma((2,)),
            dma((SIDE,)),
            dma((SIDE,)),
            dma((2 * SWEEPS,)),
            dma((2 * SWEEPS,)),
            dma((2,)),
            dma((2,)),
        ],
        compiler_params=pltpu.CompilerParams(
            collective_id=0, has_side_effects=True, vmem_limit_bytes=48 * 1024 * 1024
        ),
    )(*(pltpu.with_memory_space_constraint(a, pltpu.HBM) for a in (sample_idx.reshape(span, LANES), assign.reshape(span, LANES), counts, old_centres, precond, pool)))
    return centres, loss.reshape(row_dev)


def solution(mesh):
    return jax.shard_map(
        shards,
        mesh=mesh,
        in_specs=(
            P("dp", None),
            P("dp"),
            P("dp"),
            P("centre"),
            P("centre", "dp"),
            P("centre", "dp", None),
        ),
        out_specs=(P("centre", "dp"), P("dp")),
        check_vma=False,
    )
```

```python
import functools
import math

import jax
import jax.numpy as jnp
from jax import lax
from jax.experimental import pallas as pl
from jax.experimental.pallas import tpu as pltpu
from jax.sharding import PartitionSpec as P

D = 1024
SWEEPS = 3
CAP = 128
THRESHOLD = 0.4
EPSILON = 1e-06
ANISO = (D - 1) * THRESHOLD**2 / (1 - THRESHOLD**2)

LANES = 128
CHUNKS = D // LANES
SIDE = 4
PIECES = 1
HALF = D // 2
MESH = pl.DeviceIdType.MESH


FAR = sorted(
    [(a, b) for a in range(SIDE) for b in range(SIDE) if a or b],
    key=lambda step: -sum(min(n, SIDE - n) for n in step),
)


def iota(shape, axis):
    return lax.broadcasted_iota(jnp.int32, shape, axis)


def kernel(
    centre_count,
    mean_load,
    sample_hbm,
    assign_hbm,
    counts_hbm,
    old_hbm,
    precond_ref,
    pool_ref,
    centres_ref,
    loss_ref,
    sample_ref,
    assign_ref,
    counts_ref,
    old_ref,
    pool_buf,
    picker,
    times,
    slot_of,
    picked,
    rows_in,
    unit,
    inv_own,
    inverse,
    moment_out,
    moment_in,
    count_out,
    count_in,
    line_out,
    line_in,
    whole_out,
    whole_in,
    loss_out,
    loss_in,
    small_sem,
    pool_sem,
    own_sem,
    inv_send,
    inv_recv,
    row_send,
    row_recv,
    moment_sem,
    count_send,
    count_recv,
    line_send,
    line_recv,
    whole_sem,
    loss_sem,
):
    place = lax.axis_index("dp")
    centre = lax.axis_index("centre")
    core = lax.rem(centre, 2)
    px, pz = place // SIDE, lax.rem(place, SIDE)
    group = (1 - core) * pz + core * px
    member = (1 - core) * px + core * pz

    def device(a, b):
        m, k = lax.rem(member + a, SIDE), lax.rem(group + b, SIDE)
        return (1 - core) * (m * SIDE + k) + core * (k * SIDE + m)

    def partition(b):
        return lax.rem(group + b, SIDE)

    def pool_copy(q):
        rows = pl.ds(q * (pool_ref.shape[0] // PIECES), pool_ref.shape[0] // PIECES)
        return pltpu.make_async_copy(pool_ref.at[rows], pool_buf.at[rows], pool_sem.at[q])

    small = [
        pltpu.make_async_copy(src, dst, small_sem.at[i])
        for i, (src, dst) in enumerate(
            [(assign_hbm, assign_ref), (sample_hbm, sample_ref), (counts_hbm, counts_ref), (old_hbm, old_ref)]
        )
    ]
    for copy in small:
        copy.start()
    for q in range(PIECES):
        pool_copy(q).start()
    own_inverse = pltpu.make_async_copy(precond_ref.at[group], inverse.at[0], own_sem)
    own_inverse.start()

    barrier = pltpu.get_barrier_semaphore()
    for a, b in FAR:
        pl.semaphore_signal(barrier, inc=1, device_id=(device(a, b), centre), device_id_type=MESH)
    for k in range(1, centre_count):
        pl.semaphore_signal(
            barrier, inc=1, device_id=(place, lax.rem(centre + k, centre_count)), device_id_type=MESH
        )

    first = centre * SIDE
    small[0].wait()
    assign = assign_ref[...]
    masks = [(assign == first + k) for k in range(SIDE)]
    mask_all = jnp.concatenate([m.astype(jnp.float32) for m in masks], axis=0).astype(jnp.bfloat16)
    lane_row, lane_col = iota((LANES, LANES), 0), iota((LANES, LANES), 1)
    upper = (lane_row <= lane_col).astype(jnp.float32).astype(jnp.bfloat16)
    inside = jnp.dot(mask_all, upper, preferred_element_type=jnp.float32)
    ones = jnp.ones((LANES, LANES), jnp.bfloat16)
    totals = jnp.dot(mask_all, ones, preferred_element_type=jnp.float32)
    span = assign.shape[0]
    big_row, big_col = iota((SIDE * span, SIDE * span), 0), iota((SIDE * span, SIDE * span), 1)
    same = (big_row // span) == (big_col // span)
    before = (same & (big_col < big_row)).astype(jnp.float32).astype(jnp.bfloat16)
    ahead = jnp.dot(before, totals.astype(jnp.bfloat16), preferred_element_type=jnp.float32)
    rank = (inside + ahead).astype(jnp.int32) - 1
    for k in range(SIDE):
        slot_of[k] = jnp.where(masks[k], rank[k * span : (k + 1) * span, :], -1)
    named = [jnp.sum(totals[k * span : (k + 1) * span, :], axis=0, keepdims=True) for k in range(SIDE)]

    small[1].wait()
    sample = (sample_ref[...] + 1).astype(jnp.float32)
    slot_row = iota((CAP, LANES), 0)
    times[...] = jnp.zeros(times.shape, jnp.float32)
    indices = []
    for k in range(SIDE):
        total = jnp.zeros((CAP, LANES), jnp.float32)
        for r in range(span):
            hit = slot_of[k, r : r + 1, :] == slot_row
            total += jnp.where(hit, sample[r : r + 1, :], 0.0)
        indices.append(jnp.sum(total, axis=1, keepdims=True).astype(jnp.int32) - 1)

    def pick(t, carry):
        columns = pl.ds(pl.multiple_of(t * 256, 256), 256)
        ident = iota((CAP, 256), 1) + t * 256
        for k in range(SIDE):
            hot = (ident == indices[k]).astype(jnp.float32)
            picker[k * CAP : (k + 1) * CAP, columns] = hot.astype(jnp.bfloat16)
            times[k : k + 1, columns] = jnp.sum(hot, axis=0, keepdims=True)
        return carry

    lax.fori_loop(0, picker.shape[1] // 256, pick, 0, unroll=1)

    pl.semaphore_wait(barrier, SIDE * SIDE - 1 + centre_count - 1)
    inverse_copies = []
    for b in (2, 1, 3):
        copy = pltpu.make_async_remote_copy(
            src_ref=precond_ref.at[partition(b)],
            dst_ref=inverse.at[b],
            send_sem=inv_send.at[b],
            recv_sem=inv_recv.at[b],
            device_id=(device(0, b), centre),
            device_id_type=MESH,
        )
        copy.start()
        inverse_copies.append(copy)
    for q in range(PIECES):
        pool_copy(q).wait()
    tile_row = iota((CHUNKS, LANES), 0)
    half = lax.rem(place, 2)
    small[2].wait()
    small[3].wait()
    old = old_ref[...]
    sums = jnp.dot(times[...].astype(jnp.bfloat16), pool_buf[...], preferred_element_type=jnp.float32)
    twice = jnp.concatenate([old, old], axis=1)
    twice = jnp.where(iota(twice.shape, 1) // (LANES // 2) == half, twice, 0.0)
    for k in range(SIDE):
        rows = [sums[k : k + 1, r * LANES : (r + 1) * LANES] for r in range(CHUNKS)]
        tile = ANISO * jnp.concatenate(rows, axis=0)
        prior = counts_ref[k].astype(jnp.float32)
        tile += jnp.where(tile_row == place // 2, prior * twice[k : k + 1, :], 0.0)
        moment_out[k] = tile
        count_out[k] = jnp.broadcast_to(named[k], (CHUNKS, LANES))
    for a, b in FAR:
        pltpu.make_async_remote_copy(
            src_ref=moment_out.at[partition(b)],
            dst_ref=moment_in.at[a * SIDE + b],
            send_sem=moment_sem.at[0],
            recv_sem=moment_sem.at[1],
            device_id=(device(a, b), centre),
            device_id_type=MESH,
        ).start()

    row_copies = []
    for h in range(2):
        block = jnp.dot(picker[...], pool_buf[:, h * HALF : (h + 1) * HALF], preferred_element_type=jnp.float32)
        picked[h] = block.astype(jnp.bfloat16).reshape(SIDE, CAP, HALF)
        for b in range(1, SIDE):
            copy = pltpu.make_async_remote_copy(
                src_ref=picked.at[h, partition(b)],
                dst_ref=rows_in.at[h, b],
                send_sem=row_send.at[h, b],
                recv_sem=row_recv.at[h, b],
                device_id=(device(0, b), centre),
                device_id_type=MESH,
            )
            copy.start()
            row_copies.append(copy)
    count_copies = []
    for b in range(1, SIDE):
        copy = pltpu.make_async_remote_copy(
            src_ref=count_out.at[partition(b)],
            dst_ref=count_in.at[b],
            send_sem=count_send.at[b],
            recv_sem=count_recv.at[b],
            device_id=(device(0, b), centre),
            device_id_type=MESH,
        )
        copy.start()
        count_copies.append(copy)

    def piece(ref, part, rows, r):
        start = r % (CHUNKS // 2) * LANES
        return ref[r // (CHUNKS // 2), part, rows, start : start + LANES].astype(jnp.float32)

    def own_norm(k, carry):
        for i in range(CAP // 32):
            rows = slice(i * 32, (i + 1) * 32)
            total = jnp.zeros((32, LANES), jnp.float32)
            for r in range(CHUNKS):
                x = piece(picked, k, rows, r)
                total += x * x
            mean = jnp.sum(total, axis=1, keepdims=True) * (1.0 / D)
            inv_own[k, rows, :] = jnp.broadcast_to(lax.rsqrt(mean + EPSILON) / math.sqrt(D), (32, LANES))
        return carry

    own_inverse.wait()
    for copy in inverse_copies:
        copy.wait_recv()
    arrived = moment_in.at[pl.ds(1, SIDE * SIDE - 1)]
    pltpu.make_async_copy(arrived, arrived, moment_sem.at[1]).wait()
    moment = moment_out[group]
    for s in range(1, SIDE * SIDE):
        moment += moment_in[s]
    prior = counts_ref[group].astype(jnp.float32)
    scale = prior + mean_load
    moment = moment / scale

    block_row, block_lane = iota((64, LANES), 0), iota((64, LANES), 1)

    def apply_inverse(vector):
        tile = jnp.zeros((CHUNKS, LANES), jnp.float32)
        for b in range(SIDE):
            total = jnp.zeros((64, LANES), jnp.float32)
            for r in range(CHUNKS):
                w = inverse[b, :, r * LANES : (r + 1) * LANES].astype(jnp.float32)
                total += w * vector[r : r + 1, :]
            column = jnp.sum(total, axis=1, keepdims=True)
            home = device(0, SIDE - b)
            spread = jnp.where(block_lane == block_row + 64 * lax.rem(home, 2), column, 0.0)
            spread = jnp.sum(spread, axis=0, keepdims=True)
            tile += jnp.where(tile_row == home // 2, spread, 0.0)
        return tile

    def apply_outer(vector):
        parts = [jnp.zeros((8, LANES), jnp.float32) for _ in range(CHUNKS)]
        for i in range(SIDE * CAP // 32):
            total = jnp.zeros((32, LANES), jnp.float32)
            pieces = []
            for r in range(CHUNKS):
                u = unit[i * 32 : (i + 1) * 32, r * LANES : (r + 1) * LANES]
                pieces.append(u)
                total += u * vector[r : r + 1, :]
            along = jnp.sum(total, axis=1, keepdims=True)
            for r in range(CHUNKS):
                v = pieces[r] * along
                parts[r] += (v[0:8] + v[8:16]) + (v[16:24] + v[24:32])
        return jnp.concatenate([jnp.sum(p, axis=0, keepdims=True) for p in parts], axis=0)

    def line_sum(turn, tile):
        line_out[turn] = tile
        for a in (2, 1, 3):
            pltpu.make_async_remote_copy(
                src_ref=line_out.at[turn],
                dst_ref=line_in.at[turn, a],
                send_sem=line_send.at[turn],
                recv_sem=line_recv.at[turn],
                device_id=(device(a, 0), centre),
                device_id_type=MESH,
            ).start()
        here = line_in.at[turn, pl.ds(1, SIDE - 1)]

        def finish():
            pltpu.make_async_copy(here, here, line_recv.at[turn]).wait()
            return (tile + line_in[turn, 1]) + (line_in[turn, 2] + line_in[turn, 3])

        return finish

    finish = line_sum(0, apply_inverse(moment))

    for b in range(SIDE):
        if b:
            row_copies[b - 1].wait_recv()
            row_copies[b + SIDE - 2].wait_recv()

        for i in range(CAP // 32):
            rows = slice(i * 32, (i + 1) * 32)
            x = []
            for r in range(CHUNKS):
                x.append(piece(rows_in, b, rows, r) if b else piece(picked, group, rows, r))
            total = jnp.zeros((32, LANES), jnp.float32)
            for r in range(CHUNKS):
                total += x[r] * x[r]
            mean = jnp.sum(total, axis=1, keepdims=True) * (1.0 / D)
            inv = lax.rsqrt(mean + EPSILON) / math.sqrt(D)
            for r in range(CHUNKS):
                u = (x[r] * inv).astype(jnp.bfloat16).astype(jnp.float32)
                unit[b * CAP + i * 32 : b * CAP + (i + 1) * 32, r * LANES : (r + 1) * LANES] = u

    count = count_out[group]
    for b in range(1, SIDE):
        count_copies[b - 1].wait_recv()
        count += count_in[b]
    vector = finish()
    for sweep in range(SWEEPS):
        share = (ANISO - 1.0) * apply_outer(vector) + count * vector
        finish = line_sum(2 * sweep + 1, share)
        if sweep == 0:
            lax.fori_loop(0, SIDE, own_norm, 0)
        if sweep == SWEEPS - 1:
            lane = iota((CHUNKS, LANES), 1)
            mine = jnp.zeros((CHUNKS, LANES), jnp.float32)
            for b in range(SIDE):
                home = device(0, b)
                mine += jnp.where((tile_row == home // 2) & (lane // 64 == lax.rem(home, 2)), vector, 0.0)
        product = finish()
        slack = moment - (product + prior * vector) / scale
        change = apply_inverse(slack)
        if sweep < SWEEPS - 1:
            vector = vector + line_sum(2 * sweep + 2, change)()

    whole_out[...] = mine + change
    for a, b in FAR:
        pltpu.make_async_remote_copy(
            src_ref=whole_out,
            dst_ref=whole_in.at[a * SIDE + b],
            send_sem=whole_sem.at[0],
            recv_sem=whole_sem.at[1],
            device_id=(device(a, b), centre),
            device_id_type=MESH,
        ).start()
    arrived = whole_in.at[pl.ds(1, SIDE * SIDE - 1)]
    pltpu.make_async_copy(arrived, arrived, whole_sem.at[1]).wait()

    losses = jnp.zeros((span, LANES), jnp.float32)
    tiles = []
    part_row = iota((SIDE, LANES), 0)
    for b in range(SIDE):
        k = lax.rem(group + SIDE - b, SIDE)
        tile = whole_out[...] if b == 0 else whole_in[b]
        for a in range(1, SIDE):
            tile = tile + whole_in[a * SIDE + b]
        tiles.append((k, tile))

        columns = []
        for i in range(CAP // 32):
            rows = slice(i * 32, (i + 1) * 32)
            square = jnp.zeros((32, LANES), jnp.float32)
            along = jnp.zeros((32, LANES), jnp.float32)
            for r in range(CHUNKS):
                x = piece(picked, k, rows, r)
                deviation = x - tile[r : r + 1, :]
                square += deviation * deviation
                along += deviation * x
            along = jnp.sum(along, axis=1, keepdims=True) * inv_own[k, rows, 0:1]
            square = jnp.sum(square, axis=1, keepdims=True)
            columns.append((square + (ANISO - 1.0) * along * along) / (ANISO * D))
        column = jnp.concatenate(columns, axis=0)
        table = jnp.sum(jnp.where(lane_row == lane_col, column, 0.0), axis=0, keepdims=True)
        table = jnp.broadcast_to(table, (span, LANES))
        slots = slot_of[k]
        found = jnp.take_along_axis(table, jnp.maximum(slots, 0), axis=1)
        losses += jnp.where(slots >= 0, found, 0.0)

    loss_out[...] = losses
    for k in sorted(range(1, centre_count), key=lambda k: abs(2 * k - centre_count)):
        pltpu.make_async_remote_copy(
            src_ref=loss_out,
            dst_ref=loss_in.at[k],
            send_sem=loss_sem.at[0],
            recv_sem=loss_sem.at[1],
            device_id=(place, lax.rem(centre + k, centre_count)),
            device_id_type=MESH,
        ).start()

    centres = jnp.zeros((SIDE, LANES), jnp.float32)
    for k, tile in tiles:
        block = jnp.sum(jnp.where(tile_row == place // 2, tile, 0.0), axis=0, keepdims=True)
        centres += jnp.where(part_row == k, block, 0.0)
    swapped = jnp.concatenate([centres[:, 64:], centres[:, :64]], axis=1)
    centres_ref[...] = jnp.where(half == 0, centres, swapped)[:, :64]
    for copy in inverse_copies + row_copies + count_copies:
        copy.wait_send()
    sent = moment_in.at[pl.ds(1, SIDE * SIDE - 1)]
    pltpu.make_async_copy(sent, sent, moment_sem.at[0]).wait()
    for turn in range(2 * SWEEPS):
        sent = line_in.at[turn, pl.ds(1, SIDE - 1)]
        pltpu.make_async_copy(sent, sent, line_send.at[turn]).wait()
    sent = whole_in.at[pl.ds(1, SIDE * SIDE - 1)]
    pltpu.make_async_copy(sent, sent, whole_sem.at[0]).wait()
    if centre_count > 1:
        arrived = loss_in.at[pl.ds(1, centre_count - 1)]
        pltpu.make_async_copy(arrived, arrived, loss_sem.at[1]).wait()
        for k in range(1, centre_count):
            losses = losses + loss_in[k]
        pltpu.make_async_copy(arrived, arrived, loss_sem.at[0]).wait()
    loss_ref[...] = losses


def shards(pool, sample_idx, assign, counts, old_centres, precond):
    centre_count = lax.axis_size("centre")
    dp_count = lax.axis_size("dp")
    row_dev = sample_idx.shape[0]
    span = row_dev // LANES
    part_dev = counts.shape[0]
    mean_load = row_dev * dp_count / (part_dev * centre_count) * (D + ANISO - 1.0) / D
    pool_rows = pool.shape[0]
    f32, bf16 = jnp.float32, jnp.bfloat16
    vmem = pl.BlockSpec(memory_space=pltpu.VMEM)
    dma = pltpu.SemaphoreType.DMA
    plane = SIDE * SIDE
    centres, loss = pl.pallas_call(
        functools.partial(kernel, centre_count, mean_load),
        out_shape=(
            jax.ShapeDtypeStruct((part_dev, D // dp_count), f32),
            jax.ShapeDtypeStruct((span, LANES), f32),
        ),
        in_specs=[pl.BlockSpec(memory_space=pltpu.HBM)] * 6,
        out_specs=(vmem, vmem),
        scratch_shapes=[
            pltpu.VMEM((span, LANES), jnp.int32),
            pltpu.VMEM((span, LANES), jnp.int32),
            pltpu.SMEM((part_dev,), jnp.int32),
            pltpu.VMEM((part_dev, D // dp_count), f32),
            pltpu.VMEM((pool_rows, D), bf16),
            pltpu.VMEM((SIDE * CAP, pool_rows), bf16),
            pltpu.VMEM((8, pool_rows), f32),
            pltpu.VMEM((SIDE, span, LANES), jnp.int32),
            pltpu.VMEM((2, SIDE, CAP, HALF), bf16),
            pltpu.VMEM((2, SIDE, CAP, HALF), bf16),
            pltpu.VMEM((SIDE * CAP, D), f32),
            pltpu.VMEM((SIDE, CAP, LANES), f32),
            pltpu.VMEM((SIDE, D // dp_count, D), bf16),
            pltpu.VMEM((SIDE, CHUNKS, LANES), f32),
            pltpu.VMEM((plane, CHUNKS, LANES), f32),
            pltpu.VMEM((SIDE, CHUNKS, LANES), f32),
            pltpu.VMEM((SIDE, CHUNKS, LANES), f32),
            pltpu.VMEM((2 * SWEEPS, CHUNKS, LANES), f32),
            pltpu.VMEM((2 * SWEEPS, SIDE, CHUNKS, LANES), f32),
            pltpu.VMEM((CHUNKS, LANES), f32),
            pltpu.VMEM((plane, CHUNKS, LANES), f32),
            pltpu.VMEM((span, LANES), f32),
            pltpu.VMEM((centre_count, span, LANES), f32),
            dma((4,)),
            dma((PIECES,)),
            dma,
            dma((SIDE,)),
            dma((SIDE,)),
            dma((2, SIDE)),
            dma((2, SIDE)),
            dma((2,)),
            dma((SIDE,)),
            dma((SIDE,)),
            dma((2 * SWEEPS,)),
            dma((2 * SWEEPS,)),
            dma((2,)),
            dma((2,)),
        ],
        compiler_params=pltpu.CompilerParams(
            collective_id=0, has_side_effects=True, vmem_limit_bytes=48 * 1024 * 1024
        ),
    )(*(pltpu.with_memory_space_constraint(a, pltpu.HBM) for a in (sample_idx.reshape(span, LANES), assign.reshape(span, LANES), counts, old_centres, precond, pool)))
    return centres, loss.reshape(row_dev)


def solution(mesh):
    return jax.shard_map(
        shards,
        mesh=mesh,
        in_specs=(
            P("dp", None),
            P("dp"),
            P("dp"),
            P("centre"),
            P("centre", "dp"),
            P("centre", "dp", None),
        ),
        out_specs=(P("centre", "dp"), P("dp")),
        check_vma=False,
    )
```
